512 devices in a mesh: prompt: 8 (over y), roll: 16 (over x, z_lo, core), head: 4 (over z_hi).
Axes of the slice: x: 4, y: 8, z: 8 (z_hi: 4, z_lo: 2; z = z_hi * 2 + z_lo), core: 2. Of those that a mesh axis runs over, the one named last changes fastest.
Arguments:
- queries: bfloat16 [128, 128, 4096], P(('prompt', 'roll'), None, 'head'), parts along dimension 0, may hold values from -100 to 100
- resp_keys: bfloat16 [128, 128, 512], P(('prompt', 'roll'), None, 'head'), parts along dimension 0, may hold values from -6 to 6
- resp_values: bfloat16 [128, 128, 512], P(('prompt', 'roll'), None, 'head'), parts along dimension 0, may hold values from -6 to 6
- prefix_keys: bfloat16 [8192, 512], P(('prompt', 'roll'), 'head'), parts along dimension 0, may hold values from -4.1 to 4.1
- prefix_values: bfloat16 [8192, 512], P(('prompt', 'roll'), 'head'), parts along dimension 0, may hold values from -6 to 6
- grad_out: bfloat16 [128, 128, 4096], P(('prompt', 'roll'), None, 'head'), parts along dimension 0, may hold values from -6 to 6
- lengths: int32 [128], P(('prompt', 'roll')), parts along dimension 0, may hold values from 1 to 128, 1024 in all
Outputs:
- attended: bfloat16 [128, 128, 4096], P(('prompt', 'roll'), None, 'head'), parts along dimension 0
- query_grad: bfloat16 [128, 128, 4096], P(('prompt', 'roll'), None, 'head'), parts along dimension 0
- key_grad: bfloat16 [128, 128, 512], P(('prompt', 'roll'), None, 'head'), parts along dimension 0
- value_grad: bfloat16 [128, 128, 512], P(('prompt', 'roll'), None, 'head'), parts along dimension 0
- shared_key_grad: float32 [8192, 512], P(('prompt', 'roll'), 'head'), parts along dimension 0
- shared_value_grad: float32 [8192, 512], P(('prompt', 'roll'), 'head'), parts along dimension 0
The draws below stay inside these ranges and needn't reach their ends.
There are 8 independent parts, one for each index of `prompt`. The reference program is written for one: setup_inputs(seed, part) draws one part's arguments, and reference() takes and returns one part's arrays. A program takes and returns all parts, laid end to end along the dimension named above; each array names one. Nothing has to cross between parts.
Inputs may be any that keep to these rules, and one draw needn't show every extreme that they name: `lengths`: the longest rollout of every prompt has exactly 128 live tokens.
All inputs are finite; a program needn't handle non-finite values. No bound on the sum of `lengths` on one device may be relied on, other than what follows from the above.
Results may differ from the reference program's by a relative error of at most 0.009.
Values may be sent and summed in bfloat16 or wider, within the bound.
No kernel may reach another device: no remote copies, remote signals or barrier semaphores. Data moves between devices by JAX's collectives and lax.ppermute only.
A program may use at most 64 MiB of HBM per device.

```python
import math
import jax
import jax.numpy as jnp
import numpy as np
from jax import lax

HD = 128
QH = 32
KVH = 4
LMAX = 128
ROLLS = 16
PREFIX = 1024


def base_keys(key):
    raw_keys = jax.random.normal(jax.random.fold_in(key, 101), (PREFIX, KVH * HD), jnp.float32)
    return jnp.clip(raw_keys, -4.0, 4.0)


def draw_prefix_keys(key, part):
    shared = base_keys(key)
    return shared.astype(jnp.bfloat16)


def draw_queries(key, part):
    key = jax.random.fold_in(key, 2)
    normal_part = 2.0 * jnp.clip(jax.random.normal(key, (ROLLS, LMAX, QH * HD), jnp.float32), -4.0, 4.0)
    return normal_part.astype(jnp.bfloat16)


def level_of(stream_key, extent, shards, low, high):
    loudness, own = 1.0, jax.random.fold_in(stream_key, 6)
    for position, parts in shards:
        heights = jnp.exp(jax.random.uniform(jax.random.fold_in(own, position), (parts,), jnp.float32, low / len(shards), high / len(shards)))
        loudness = loudness * jnp.repeat(heights, extent[position] // parts).reshape([-1 if axis == position else 1 for axis in range(len(extent))])
    return loudness


def length_profile(number_of, total, reach, slope):
    portions = [(1 << 20) // math.isqrt(rank ** slope) + 1 for rank in range(2, number_of + 1)]
    spare, counts = total - reach - (number_of - 1), [1] * (number_of - 1)
    while spare > 0:
        free = [i for i in range(number_of - 1) if counts[i] < reach]
        mass, budget = sum([portions[i] for i in free]), spare
        for i in free:
            extra = min(reach - counts[i], max(1, budget * portions[i] // mass), spare)
            counts[i] = counts[i] + extra
            spare = spare - extra
    return np.array([reach] + counts)


def ragged_sizes(stream_key, count, total, limit, slope):
    if count == 2:
        one = jax.random.randint(stream_key, (), max(1, total - limit), min(limit, total - 1) + 1)
        return jnp.stack([one, total - one])
    sizes = jnp.asarray(length_profile(count, total, limit, slope), jnp.int32)
    pairs = (count - 1) // 2
    donor, receiver = sizes[1:1 + 2 * pairs:2], sizes[2:2 + 2 * pairs:2]
    margin = jnp.minimum(donor - 1, limit - receiver)
    moved = jax.random.randint(jax.random.fold_in(stream_key, 1), (pairs,), 0, 1 << 20) % (margin + 1)
    sizes = sizes.at[1:1 + 2 * pairs:2].set(donor - moved).at[2:2 + 2 * pairs:2].set(receiver + moved)
    return sizes[jax.random.permutation(jax.random.fold_in(stream_key, 2), count)]


def noise(own_key, extent, scale, most, cuts=(), kind=jnp.bfloat16):
    result = jax.random.normal(own_key, extent, jnp.float32) * scale
    if len(cuts) > 0:
        result = level_of(own_key, extent, cuts, -0.22, 0.18) * result
    return jnp.clip(result, min=-most, max=most).astype(kind)


def setup_inputs(seed: int = 0, part: int = 0) -> dict:
    key_of = jax.random.split(jax.random.key(seed), 8)
    own_keys = jax.random.split(jax.random.fold_in(key_of[7], part), 8)
    return {
        "queries": draw_queries(jax.random.fold_in(jax.random.fold_in(key_of[7], part), 71), part),
        "resp_keys": noise(own_keys[1], (ROLLS, LMAX, KVH * HD), 1.0, 6.0, ((0, 16), (2, 4))),
        "resp_values": noise(own_keys[2], (ROLLS, LMAX, KVH * HD), 1.0, 6.0, ((0, 16), (2, 4))),
        "prefix_keys": draw_prefix_keys(jax.random.fold_in(jax.random.fold_in(key_of[7], part), 71), part),
        "prefix_values": noise(own_keys[4], (PREFIX, KVH * HD), 1.0, 6.0, ((0, 16), (1, 4))),
        "grad_out": noise(own_keys[5], (ROLLS, LMAX, QH * HD), 1.0, 6.0, ((0, 16), (2, 4))),
        "lengths": ragged_sizes(own_keys[6], ROLLS, ROLLS * LMAX // 2, LMAX, 2).astype(jnp.int32),
    }


masked_score = -1e+30

def widen(array):
    return lax.optimization_barrier(array.astype(jnp.bfloat16)).astype(jnp.float32)

def one_rollout(shared_keys, shared_values, rollout):
    queries, resp_keys, resp_values, grad_out, length = rollout
    group_size = QH // KVH
    factor = 1.0 / math.sqrt(HD)
    query_full = queries.astype(jnp.float32).reshape(LMAX, KVH, group_size, HD)
    key_full = jnp.concatenate([shared_keys, resp_keys], axis=0).astype(jnp.float32).reshape(PREFIX + LMAX, KVH, HD)
    value_full = jnp.concatenate([shared_values, resp_values], axis=0).astype(jnp.float32).reshape(PREFIX + LMAX, KVH, HD)
    token_index = jnp.arange(LMAX, dtype=jnp.int32)[:, None]
    key_index = jnp.arange(PREFIX + LMAX, dtype=jnp.int32)[None, :] - PREFIX
    allowed = (key_index < 0) | (key_index <= token_index) & (key_index < length)
    scores = jnp.einsum('tkgd,skd->kgts', query_full, key_full) * factor
    scores = jnp.where(allowed, scores, masked_score)
    row_max = lax.optimization_barrier(jnp.max(scores, axis=-1, keepdims=True))
    exponent = jnp.exp(scores - row_max)
    probability = exponent / lax.optimization_barrier(jnp.sum(exponent, axis=-1, keepdims=True))
    rounded = widen(probability)
    living = jnp.arange(LMAX, dtype=jnp.int32) < length
    outputs = jnp.einsum('kgts,skd->tkgd', rounded, value_full)
    attended = jnp.where(living[:, None, None, None], outputs, 0.0).astype(jnp.bfloat16).reshape(LMAX, QH * HD)
    cotangent = jnp.where(living[:, None], grad_out, jnp.zeros_like(grad_out))
    cotangent_full = cotangent.astype(jnp.float32).reshape(LMAX, KVH, group_size, HD)
    grad_weights = jnp.einsum('tkgd,skd->kgts', cotangent_full, value_full)
    correction = lax.optimization_barrier(jnp.sum(probability * grad_weights, axis=-1, keepdims=True))
    grad_scores = widen(probability * (grad_weights - correction) * factor)
    query_grad = jnp.einsum('kgts,skd->tkgd', grad_scores, key_full).astype(jnp.bfloat16).reshape(LMAX, QH * HD)
    key_terms = jnp.einsum('kgts,tkgd->skd', grad_scores, query_full).reshape(PREFIX + LMAX, KVH * HD)
    value_terms = jnp.einsum('kgts,tkgd->skd', rounded, cotangent_full).reshape(PREFIX + LMAX, KVH * HD)
    return (attended, query_grad, key_terms[PREFIX:].astype(jnp.bfloat16), value_terms[PREFIX:].astype(jnp.bfloat16), key_terms[:PREFIX], value_terms[:PREFIX])

def reference(queries, resp_keys, resp_values, prefix_keys, prefix_values, grad_out, lengths):

    def advance(carried, rollout):
        pieces = one_rollout(prefix_keys, prefix_values, rollout)
        return ((carried[0] + pieces[4], carried[1] + pieces[5]), (pieces[0], pieces[1], pieces[2], pieces[3]))
    initial = (jnp.zeros((PREFIX, KVH * HD), jnp.float32), jnp.zeros((PREFIX, KVH * HD), jnp.float32))
    totals, stacked = lax.scan(advance, initial, (queries, resp_keys, resp_values, grad_out, lengths.astype(jnp.int32)))
    return (stacked[0], stacked[1], stacked[2], stacked[3], totals[0], totals[1])
```

```python
import functools
import math

import jax
import jax.numpy as jnp
from jax import lax
from jax.experimental import pallas as pl
from jax.experimental.pallas import tpu as pltpu
from jax.sharding import PartitionSpec as P

masked_score = -1e30


def contract(left, right, dims):
    return lax.dot_general(
        left, right, ((dims[:1], dims[1:]), ((), ())), preferred_element_type=jnp.float32
    )


def spread_kernel(key_ref, value_ref, out_ref):
    head_size = key_ref.shape[1]
    for place in range(out_ref.shape[0]):
        out_ref[place, :, :head_size] = key_ref[...]
        out_ref[place, :, head_size:] = value_ref[...]


def total_kernel(pieces_ref, key_ref, value_ref):
    head_size = key_ref.shape[1]
    total = pieces_ref[0].astype(jnp.float32)
    for place in range(1, pieces_ref.shape[0]):
        total = total + pieces_ref[place].astype(jnp.float32)
    key_ref[...] = total[:, :head_size]
    value_ref[...] = total[:, head_size:]


def attention_kernel(
    length_ref,
    core_ref,
    query_ref,
    grad_ref,
    near_ref,
    far_ref,
    resp_key_ref,
    resp_value_ref,
    attended_ref,
    query_grad_ref,
    key_grad_ref,
    value_grad_ref,
    share_ref,
    key_rows,
    value_rows,
    key_sum,
    value_sum,
):
    tokens, head_size = resp_key_ref.shape
    half = near_ref.shape[0]
    prompt = 2 * half
    heads = query_ref.shape[1] // head_size
    factor = 1.0 / math.sqrt(head_size)
    exponent_factor = factor * math.log2(math.e)
    length = length_ref[0]

    for place, part_ref in enumerate((near_ref, far_ref)):
        span = slice(place * half, (place + 1) * half)
        key_rows[span] = part_ref[:, :head_size]
        value_rows[span, :head_size] = part_ref[:, head_size:]
    key_rows[prompt:] = resp_key_ref[...]
    value_rows[prompt:, :head_size] = resp_value_ref[...]
    value_rows[:, head_size:] = jnp.ones((prompt + tokens, head_size), jnp.bfloat16)

    pair = 2
    rows = pair * tokens
    token = lax.broadcasted_iota(jnp.int32, (rows, tokens), 0) % tokens
    slot = lax.broadcasted_iota(jnp.int32, (rows, tokens), 1)
    allowed = (slot <= token) & (slot < length)
    living = token < length

    for first in range(0, heads, pair):
        spans = [slice(h * head_size, (h + 1) * head_size) for h in range(first, first + pair)]
        query = jnp.concatenate([query_ref[:, span] for span in spans], axis=0)
        grad = jnp.concatenate([grad_ref[:, span] for span in spans], axis=0)
        scores = contract(query, key_rows[...], (1, 1))
        own = jnp.where(allowed, scores[:, prompt:], masked_score)
        scores = jnp.concatenate([scores[:, :prompt], own], axis=1)
        row_max = jnp.max(scores, axis=1, keepdims=True)
        weights = jnp.exp2((scores - row_max) * exponent_factor).astype(jnp.bfloat16)
        sums = contract(weights, value_rows[...], (1, 0))
        inverse = 1.0 / sums[:, head_size:]
        outputs = sums[:, :head_size] * inverse
        attended = jnp.where(living, outputs, 0.0).astype(jnp.bfloat16)
        grad = jnp.where(living, grad.astype(jnp.float32) * inverse, 0.0).astype(jnp.bfloat16)
        correction = jnp.sum(grad.astype(jnp.float32) * outputs, axis=1, keepdims=True)
        grad_weights = contract(grad, value_rows[:, :head_size], (1, 1))
        grad_scores = (weights.astype(jnp.float32) * (grad_weights - correction)).astype(jnp.bfloat16)
        query_grad = (contract(grad_scores, key_rows[...], (1, 0)) * factor).astype(jnp.bfloat16)
        for place, span in enumerate(spans):
            part = slice(place * tokens, (place + 1) * tokens)
            attended_ref[:, span] = attended[part]
            query_grad_ref[:, span] = query_grad[part]
        key_part = contract(query, grad_scores, (0, 0))
        value_part = contract(grad, weights, (0, 0))
        if first == 0:
            key_sum[...] = key_part
            value_sum[...] = value_part
        else:
            key_sum[...] += key_part
            value_sum[...] += value_part

    key_total = (key_sum[...] * factor).astype(jnp.bfloat16).T
    value_total = value_sum[...].astype(jnp.bfloat16).T
    key_grad_ref[...] = key_total[prompt:]
    value_grad_ref[...] = value_total[prompt:]
    owned = share_ref.shape[1]
    core = core_ref[0]
    for place in range(prompt // owned):
        side, chip = divmod(place, half // owned)
        rank = 2 * chip + (core if side == 0 else 1 - core)
        span = slice(place * owned, (place + 1) * owned)
        share_ref[rank, :, :head_size] = key_total[span]
        share_ref[rank, :, head_size:] = value_total[span]


def attention(length, core, queries, grads, near, far, resp_keys, resp_values, owned):
    tokens, head_size = resp_keys.shape
    prompt = 2 * near.shape[0]
    key_count = prompt + tokens
    vmem = pl.BlockSpec(memory_space=pltpu.VMEM)
    return pl.pallas_call(
        attention_kernel,
        out_shape=(
            jax.ShapeDtypeStruct(queries.shape, jnp.bfloat16),
            jax.ShapeDtypeStruct(queries.shape, jnp.bfloat16),
            jax.ShapeDtypeStruct(resp_keys.shape, jnp.bfloat16),
            jax.ShapeDtypeStruct(resp_keys.shape, jnp.bfloat16),
            jax.ShapeDtypeStruct((prompt // owned, owned, 2 * head_size), jnp.bfloat16),
        ),
        in_specs=[pl.BlockSpec(memory_space=pltpu.SMEM)] * 2 + [vmem] * 6,
        out_specs=[vmem] * 5,
        scratch_shapes=[
            pltpu.VMEM((key_count, head_size), jnp.bfloat16),
            pltpu.VMEM((key_count, 2 * head_size), jnp.bfloat16),
            pltpu.VMEM((head_size, key_count), jnp.float32),
            pltpu.VMEM((head_size, key_count), jnp.float32),
        ],
        compiler_params=pltpu.CompilerParams(vmem_limit_bytes=48 * 1024 * 1024),
    )(length, core, queries, grads, near, far, resp_keys, resp_values)


def on_device(ranks, queries, resp_keys, resp_values, prefix_keys, prefix_values, grad_out, lengths):
    head_size = resp_keys.shape[2]
    owned = prefix_keys.shape[0]
    chips = ranks // 2
    vmem = pl.BlockSpec(memory_space=pltpu.VMEM)
    sent = pl.pallas_call(
        spread_kernel,
        out_shape=jax.ShapeDtypeStruct((chips, owned, 2 * head_size), jnp.bfloat16),
        in_specs=[vmem] * 2,
        out_specs=vmem,
    )(prefix_keys, prefix_values)
    same_core = [list(range(core, ranks, 2)) for core in range(2)]
    near = lax.all_to_all(sent, "roll", 0, 0, axis_index_groups=same_core)
    near = near.reshape(chips * owned, 2 * head_size)
    far = lax.ppermute(near, "roll", [(rank, rank ^ 1) for rank in range(ranks)])
    core = (lax.axis_index("roll") % 2).astype(jnp.int32)[None]
    attended, query_grad, key_grad, value_grad, share = attention(
        lengths, core, queries[0], grad_out[0], near, far, resp_keys[0], resp_values[0], owned
    )
    pieces = lax.all_to_all(share, "roll", 0, 0)
    key_total, value_total = pl.pallas_call(
        total_kernel,
        out_shape=(jax.ShapeDtypeStruct((owned, head_size), jnp.float32),) * 2,
        in_specs=[vmem],
        out_specs=[vmem] * 2,
    )(pieces)
    return (
        attended[None],
        query_grad[None],
        key_grad[None],
        value_grad[None],
        key_total,
        value_total,
    )


def solution(mesh):
    rolls = P(("prompt", "roll"), None, "head")
    prompts = P(("prompt", "roll"), "head")
    return jax.shard_map(
        functools.partial(on_device, mesh.shape["roll"]),
        mesh=mesh,
        in_specs=(rolls, rolls, rolls, prompts, prompts, rolls, P(("prompt", "roll"))),
        out_specs=(rolls, rolls, rolls, rolls, prompts, prompts),
        check_vma=False,
    )
```

```python
import functools
import math

import jax
import jax.numpy as jnp
from jax import lax
from jax.experimental import pallas as pl
from jax.experimental.pallas import tpu as pltpu
from jax.sharding import PartitionSpec as P

masked_score = -1e30


def contract(left, right, dims):
    return lax.dot_general(
        left, right, ((dims[:1], dims[1:]), ((), ())), preferred_element_type=jnp.float32
    )


def attention_kernel(
    length_ref,
    query_ref,
    grad_ref,
    prefix_ref,
    resp_key_ref,
    resp_value_ref,
    attended_ref,
    query_grad_ref,
    key_grad_ref,
    value_grad_ref,
    share_ref,
    key_rows,
    value_rows,
    key_sum,
    value_sum,
):
    tokens, head_size = resp_key_ref.shape
    ranks, owned, _ = prefix_ref.shape
    prompt = ranks * owned
    heads = query_ref.shape[1] // head_size
    factor = 1.0 / math.sqrt(head_size)
    exponent_factor = factor * math.log2(math.e)
    length = length_ref[0]

    for rank in range(ranks):
        span = slice(rank * owned, (rank + 1) * owned)
        key_rows[span] = prefix_ref[rank, :, :head_size]
        value_rows[span, :head_size] = prefix_ref[rank, :, head_size:]
    key_rows[prompt:] = resp_key_ref[...]
    value_rows[prompt:, :head_size] = resp_value_ref[...]
    value_rows[:, head_size:] = jnp.ones((prompt + tokens, head_size), jnp.bfloat16)
    key_sum[...] = jnp.zeros_like(key_sum)
    value_sum[...] = jnp.zeros_like(value_sum)

    pair = 2
    rows = pair * tokens
    token = lax.broadcasted_iota(jnp.int32, (rows, tokens), 0) % tokens
    slot = lax.broadcasted_iota(jnp.int32, (rows, tokens), 1)
    allowed = (slot <= token) & (slot < length)
    living = token < length

    @pl.loop(0, heads, step=pair)
    def _(first):
        spans = [
            pl.ds(pl.multiple_of((first + place) * head_size, head_size), head_size)
            for place in range(pair)
        ]
        query = jnp.concatenate([query_ref[:, span] for span in spans], axis=0)
        grad = jnp.concatenate([grad_ref[:, span] for span in spans], axis=0)
        scores = contract(query, key_rows[...], (1, 1))
        own = jnp.where(allowed, scores[:, prompt:], masked_score)
        scores = jnp.concatenate([scores[:, :prompt], own], axis=1)
        row_max = jnp.max(scores, axis=1, keepdims=True)
        weights = jnp.exp2((scores - row_max) * exponent_factor).astype(jnp.bfloat16)
        sums = contract(weights, value_rows[...], (1, 0))
        inverse = 1.0 / sums[:, head_size:]
        outputs = sums[:, :head_size] * inverse
        attended = jnp.where(living, outputs, 0.0).astype(jnp.bfloat16)
        grad = jnp.where(living, grad.astype(jnp.float32) * inverse, 0.0).astype(jnp.bfloat16)
        correction = jnp.sum(grad.astype(jnp.float32) * outputs, axis=1, keepdims=True)
        grad_weights = contract(grad, value_rows[:, :head_size], (1, 1))
        grad_scores = (weights.astype(jnp.float32) * (grad_weights - correction)).astype(jnp.bfloat16)
        query_grad = (contract(grad_scores, key_rows[...], (1, 0)) * factor).astype(jnp.bfloat16)
        for place, span in enumerate(spans):
            part = slice(place * tokens, (place + 1) * tokens)
            attended_ref[:, span] = attended[part]
            query_grad_ref[:, span] = query_grad[part]
        key_sum[...] += contract(query, grad_scores, (0, 0))
        value_sum[...] += contract(grad, weights, (0, 0))

    key_total = (key_sum[...] * factor).astype(jnp.bfloat16).T
    value_total = value_sum[...].astype(jnp.bfloat16).T
    key_grad_ref[...] = key_total[prompt:]
    value_grad_ref[...] = value_total[prompt:]
    for rank in range(ranks):
        span = slice(rank * owned, (rank + 1) * owned)
        share_ref[rank, :, :head_size] = key_total[span]
        share_ref[rank, :, head_size:] = value_total[span]


def attention(length, queries, grads, prefix, resp_keys, resp_values):
    tokens, head_size = resp_keys.shape
    key_count = prefix.shape[0] * prefix.shape[1] + tokens
    vmem = pl.BlockSpec(memory_space=pltpu.VMEM)
    return pl.pallas_call(
        attention_kernel,
        out_shape=(
            jax.ShapeDtypeStruct(queries.shape, jnp.bfloat16),
            jax.ShapeDtypeStruct(queries.shape, jnp.bfloat16),
            jax.ShapeDtypeStruct(resp_keys.shape, jnp.bfloat16),
            jax.ShapeDtypeStruct(resp_keys.shape, jnp.bfloat16),
            jax.ShapeDtypeStruct(prefix.shape, jnp.bfloat16),
        ),
        in_specs=[pl.BlockSpec(memory_space=pltpu.SMEM)] + [vmem] * 5,
        out_specs=[vmem] * 5,
        scratch_shapes=[
            pltpu.VMEM((key_count, head_size), jnp.bfloat16),
            pltpu.VMEM((key_count, 2 * head_size), jnp.bfloat16),
            pltpu.VMEM((head_size, key_count), jnp.float32),
            pltpu.VMEM((head_size, key_count), jnp.float32),
        ],
        compiler_params=pltpu.CompilerParams(vmem_limit_bytes=48 * 1024 * 1024),
    )(length, queries, grads, prefix, resp_keys, resp_values)


def on_device(ranks, queries, resp_keys, resp_values, prefix_keys, prefix_values, grad_out, lengths):
    head_size = resp_keys.shape[2]
    own = jnp.concatenate([prefix_keys, prefix_values], axis=1)
    sent = jnp.broadcast_to(own[None], (ranks, *own.shape))
    prefix = lax.all_to_all(sent, "roll", 0, 0)
    attended, query_grad, key_grad, value_grad, share = attention(
        lengths, queries[0], grad_out[0], prefix, resp_keys[0], resp_values[0]
    )
    pieces = lax.all_to_all(share, "roll", 0, 0)
    total = pieces[0].astype(jnp.float32)
    for rank in range(1, ranks):
        total = total + pieces[rank].astype(jnp.float32)
    return (
        attended[None],
        query_grad[None],
        key_grad[None],
        value_grad[None],
        total[:, :head_size],
        total[:, head_size:],
    )


def solution(mesh):
    rolls = P(("prompt", "roll"), None, "head")
    prompts = P(("prompt", "roll"), "head")
    return jax.shard_map(
        functools.partial(on_device, mesh.shape["roll"]),
        mesh=mesh,
        in_specs=(rolls, rolls, rolls, prompts, prompts, rolls, P(("prompt", "roll"))),
        out_specs=(rolls, rolls, rolls, rolls, prompts, prompts),
        check_vma=False,
    )
```

```python
import functools
import math

import jax
import jax.numpy as jnp
from jax import lax
from jax.experimental import pallas as pl
from jax.experimental.pallas import tpu as pltpu
from jax.sharding import PartitionSpec as P

masked_score = -1e30
GROUP = 4


def contract(left, right, dims):
    return lax.dot_general(
        left, right, ((dims[:1], dims[1:]), ((), ())), preferred_element_type=jnp.float32
    )


def head_parts(columns, tokens, head_size):
    return [
        (slice(head * tokens, (head + 1) * tokens), slice(head * head_size, (head + 1) * head_size))
        for head in range(columns // head_size)
    ]


def spread_kernel(length_ref, key_hbm, value_hbm, out_ref, living_ref, own, sems):
    head_size = key_hbm.shape[1]
    copies = [
        pltpu.make_async_copy(source, own.at[place], sems.at[place])
        for place, source in enumerate((key_hbm, value_hbm))
    ]
    for copy in copies:
        copy.start()
    token = lax.broadcasted_iota(jnp.int32, living_ref.shape, 0)
    living_ref[...] = (token < length_ref[0]).astype(jnp.float32)
    for copy in copies:
        copy.wait()
    for place in range(out_ref.shape[0]):
        out_ref[place, :, :head_size] = own[0]
        out_ref[place, :, head_size:] = own[1]


def attention_kernel(
    living_ref,
    query_ref,
    grad_ref,
    resp_key_ref,
    resp_value_ref,
    prefix_ref,
    attended_hbm,
    query_grad_hbm,
    key_grad_hbm,
    value_grad_hbm,
    share_ref,
    key_rows,
    value_rows,
    attended_ref,
    query_grad_ref,
    own_grad_ref,
    sems,
):
    tokens, head_size = resp_key_ref.shape
    ranks, owned, _ = prefix_ref.shape
    prompt = ranks * owned
    heads = query_ref.shape[1] // head_size
    factor = 1.0 / math.sqrt(head_size)
    exponent_factor = factor * math.log2(math.e)
    parts = head_parts(query_ref.shape[1], tokens, head_size)
    copies = []

    def send(source, target):
        copy = pltpu.make_async_copy(source, target, sems.at[len(copies)])
        copy.start()
        copies.append(copy)

    for rank in range(ranks):
        span = slice(rank * owned, (rank + 1) * owned)
        key_rows[span] = prefix_ref[rank, :, :head_size]
        value_rows[span, :head_size] = prefix_ref[rank, :, head_size:]
    key_rows[prompt:] = resp_key_ref[...]
    value_rows[prompt:, :head_size] = resp_value_ref[...]
    value_rows[:, head_size:] = jnp.ones((prompt + tokens, head_size), jnp.bfloat16)

    groups = [parts[at : at + GROUP] for at in range(0, heads, GROUP)]
    stacked = [
        [jnp.concatenate([ref[:, span] for _, span in group], axis=0) for group in groups]
        for ref in (query_ref, grad_ref)
    ]
    queries, grads = stacked
    living = jnp.concatenate([living_ref[...]] * GROUP, axis=0) > 0.0
    token = lax.broadcasted_iota(jnp.int32, (GROUP * tokens, tokens), 0) % tokens
    allowed = lax.broadcasted_iota(jnp.int32, (GROUP * tokens, tokens), 1) <= token

    def exponentials(scores):
        own = jnp.where(allowed, scores[:, prompt:], masked_score)
        scores = jnp.concatenate([scores[:, :prompt], own], axis=1)
        row_max = jnp.max(scores, axis=1, keepdims=True)
        return jnp.exp2((scores - row_max) * exponent_factor).astype(jnp.bfloat16)

    def normalised(index, sums):
        inverse = 1.0 / sums[:, head_size:]
        outputs = sums[:, :head_size] * inverse
        attended = jnp.where(living, outputs, 0.0).astype(jnp.bfloat16)
        for place, (_, span) in enumerate(groups[index]):
            attended_ref[:, span] = attended[place * tokens : (place + 1) * tokens]
        grad = jnp.where(living, grads[index].astype(jnp.float32) * inverse, 0.0).astype(jnp.bfloat16)
        return grad, jnp.sum(grad.astype(jnp.float32) * outputs, axis=1, keepdims=True)

    count = len(groups)
    scores, weights, sums, states, grad_weights, grad_scores = ([None] * count for _ in range(6))
    for step in range(count + 1):
        if step < count:
            scores[step] = contract(queries[step], key_rows[...], (1, 1))
        if step > 0:
            weights[step - 1] = exponentials(scores[step - 1])
            sums[step - 1] = contract(weights[step - 1], value_rows[...], (1, 0))
    for step in range(count + 1):
        if step < count:
            states[step] = normalised(step, sums[step])
            grad_weights[step] = contract(states[step][0], value_rows[:, :head_size], (1, 1))
        if step > 0:
            last = step - 1
            shifted = (grad_weights[last] - states[last][1]).astype(jnp.bfloat16)
            grad_scores[last] = weights[last] * shifted
            query_grad = contract(grad_scores[last], key_rows[...], (1, 0)) * factor
            for place, (_, span) in enumerate(groups[last]):
                part = query_grad[place * tokens : (place + 1) * tokens]
                query_grad_ref[:, span] = part.astype(jnp.bfloat16)
    send(attended_ref, attended_hbm)
    query = jnp.concatenate(queries, axis=0)
    grad = jnp.concatenate([state[0] for state in states], axis=0)
    weights = jnp.concatenate(weights, axis=0)
    grad_scores = jnp.concatenate(grad_scores, axis=0)
    send(query_grad_ref, query_grad_hbm)
    key_total = (contract(query, grad_scores, (0, 0)) * factor).astype(jnp.bfloat16)
    value_total = contract(grad, weights, (0, 0)).astype(jnp.bfloat16)
    own_grad_ref[0] = key_total[:, prompt:].T
    send(own_grad_ref.at[0], key_grad_hbm)
    own_grad_ref[1] = value_total[:, prompt:].T
    send(own_grad_ref.at[1], value_grad_hbm)
    for place, total in enumerate((key_total, value_total)):
        turned = total[:, :prompt].T
        for rank in range(ranks):
            lanes = slice(place * head_size, (place + 1) * head_size)
            share_ref[rank, :, lanes] = turned[rank * owned : (rank + 1) * owned]
    for copy in copies:
        copy.wait()


def on_device(ranks, queries, resp_keys, resp_values, prefix_keys, prefix_values, grad_out, lengths):
    tokens, columns = queries.shape[1:]
    owned, head_size = prefix_keys.shape
    key_count = ranks * owned + tokens
    half = jnp.bfloat16
    vmem = pl.BlockSpec(memory_space=pltpu.VMEM)
    anywhere = pl.BlockSpec(memory_space=pl.ANY)

    sent, living = pl.pallas_call(
        spread_kernel,
        out_shape=(
            pltpu.VMEM((ranks, owned, 2 * head_size), half),
            pltpu.VMEM((tokens, head_size), jnp.float32),
        ),
        in_specs=[pl.BlockSpec(memory_space=pltpu.SMEM)] + [pl.BlockSpec(memory_space=pltpu.HBM)] * 2,
        out_specs=[vmem] * 2,
        scratch_shapes=[pltpu.VMEM((2, owned, head_size), half), pltpu.SemaphoreType.DMA((2,))],
    )(lengths, prefix_keys, prefix_values)
    prefix = lax.all_to_all(sent, "roll", 0, 0)
    attended, query_grad, key_grad, value_grad, share = pl.pallas_call(
        attention_kernel,
        out_shape=(
            jax.ShapeDtypeStruct((tokens, columns), half),
            jax.ShapeDtypeStruct((tokens, columns), half),
            jax.ShapeDtypeStruct((tokens, head_size), half),
            jax.ShapeDtypeStruct((tokens, head_size), half),
            pltpu.VMEM((ranks, owned, 2 * head_size), half),
        ),
        in_specs=[vmem] * 6,
        out_specs=[anywhere] * 4 + [vmem],
        scratch_shapes=[
            pltpu.VMEM((key_count, head_size), half),
            pltpu.VMEM((key_count, 2 * head_size), half),
            pltpu.VMEM((tokens, columns), half),
            pltpu.VMEM((tokens, columns), half),
            pltpu.VMEM((2, tokens, head_size), half),
            pltpu.SemaphoreType.DMA((4,)),
        ],
        compiler_params=pltpu.CompilerParams(vmem_limit_bytes=48 * 1024 * 1024),
    )(living, queries[0], grad_out[0], resp_keys[0], resp_values[0], prefix)
    pieces = lax.all_to_all(share, "roll", 0, 0)
    total = pieces[0].astype(jnp.float32)
    for rank in range(1, ranks):
        total = total + pieces[rank].astype(jnp.float32)
    return (
        attended[None],
        query_grad[None],
        key_grad[None],
        value_grad[None],
        total[:, :head_size],
        total[:, head_size:],
    )


def solution(mesh):
    rolls = P(("prompt", "roll"), None, "head")
    prompts = P(("prompt", "roll"), "head")
    return jax.shard_map(
        functools.partial(on_device, mesh.shape["roll"]),
        mesh=mesh,
        in_specs=(rolls, rolls, rolls, prompts, prompts, rolls, P(("prompt", "roll"))),
        out_specs=(rolls, rolls, rolls, rolls, prompts, prompts),
        check_vma=False,
    )
```

```python
import functools
import math

import jax
import jax.numpy as jnp
from jax import lax
from jax.experimental import pallas as pl
from jax.experimental.pallas import tpu as pltpu
from jax.sharding import PartitionSpec as P

masked_score = -1e30
GROUP = 4


def contract(left, right, dims):
    return lax.dot_general(
        left, right, ((dims[:1], dims[1:]), ((), ())), preferred_element_type=jnp.float32
    )


def head_parts(columns, tokens, head_size):
    return [
        (slice(head * tokens, (head + 1) * tokens), slice(head * head_size, (head + 1) * head_size))
        for head in range(columns // head_size)
    ]


def spread_kernel(length_ref, key_hbm, value_hbm, out_ref, living_ref, own, sems):
    head_size = key_hbm.shape[1]
    copies = [
        pltpu.make_async_copy(source, own.at[place], sems.at[place])
        for place, source in enumerate((key_hbm, value_hbm))
    ]
    for copy in copies:
        copy.start()
    token = lax.broadcasted_iota(jnp.int32, living_ref.shape, 0)
    living_ref[...] = (token < length_ref[0]).astype(jnp.float32)
    for copy in copies:
        copy.wait()
    for place in range(out_ref.shape[0]):
        out_ref[place, :, :head_size] = own[0]
        out_ref[place, :, head_size:] = own[1]


def near_kernel(
    query_hbm,
    grad_hbm,
    resp_key_hbm,
    resp_value_hbm,
    near_ref,
    query_rows_ref,
    grad_ref,
    own_ref,
    scores_ref,
    query_ref,
    sems,
):
    tokens, head_size = own_ref.shape[1:]
    moves = (
        (query_hbm, query_ref),
        (grad_hbm, grad_ref),
        (resp_key_hbm, own_ref.at[0]),
        (resp_value_hbm, own_ref.at[1]),
    )
    copies = [
        pltpu.make_async_copy(source, target, sems.at[place])
        for place, (source, target) in enumerate(moves)
    ]
    for copy in copies:
        copy.start()
    keys = jnp.concatenate([near_ref[place, :, :head_size] for place in range(near_ref.shape[0])], axis=0)
    copies[0].wait()
    for rows, span in head_parts(query_ref.shape[1], tokens, head_size):
        query = query_ref[:, span]
        query_rows_ref[rows] = query
        scores_ref[rows] = contract(query, keys, (1, 1))
    for copy in copies[1:]:
        copy.wait()


def attention_kernel(
    living_ref,
    query_rows_ref,
    grad_ref,
    own_ref,
    near_ref,
    far_ref,
    near_scores_ref,
    attended_hbm,
    weights_ref,
    grad_scores_ref,
    grad_rows_ref,
    key_rows,
    far_share_ref,
    value_rows,
    attended_ref,
    sem,
):
    tokens, head_size = own_ref.shape[1:]
    chips, owned, _ = near_ref.shape
    half = chips * owned
    prompt = 2 * half
    heads = grad_ref.shape[1] // head_size
    factor = 1.0 / math.sqrt(head_size)
    exponent_factor = factor * math.log2(math.e)
    parts = head_parts(grad_ref.shape[1], tokens, head_size)
    for side, part_ref in enumerate((near_ref, far_ref)):
        for chip in range(chips):
            span = slice(side * half + chip * owned, side * half + (chip + 1) * owned)
            key_rows[span] = part_ref[chip, :, :head_size]
            value_rows[span, :head_size] = part_ref[chip, :, head_size:]
    key_rows[prompt:] = own_ref[0]
    value_rows[prompt:, :head_size] = own_ref[1]
    value_rows[:, head_size:] = jnp.ones((prompt + tokens, head_size), jnp.bfloat16)

    groups = [parts[at : at + GROUP] for at in range(0, heads, GROUP)]
    queries = [query_rows_ref[at * tokens : (at + GROUP) * tokens] for at in range(0, heads, GROUP)]
    grads = [jnp.concatenate([grad_ref[:, span] for _, span in group], axis=0) for group in groups]
    living = jnp.concatenate([living_ref[...]] * GROUP, axis=0) > 0.0
    token = lax.broadcasted_iota(jnp.int32, (GROUP * tokens, tokens), 0) % tokens
    allowed = lax.broadcasted_iota(jnp.int32, (GROUP * tokens, tokens), 1) <= token

    def exponentials(near, scores):
        own = jnp.where(allowed, scores[:, half:], masked_score)
        parts = (near, scores[:, :half], own)
        row_max = functools.reduce(jnp.maximum, [jnp.max(part, axis=1, keepdims=True) for part in parts])
        return jnp.concatenate(
            [jnp.exp2((part - row_max) * exponent_factor).astype(jnp.bfloat16) for part in parts], axis=1
        )

    def normalised(index, sums):
        inverse = 1.0 / sums[:, head_size:]
        outputs = sums[:, :head_size] * inverse
        attended = jnp.where(living, outputs, 0.0).astype(jnp.bfloat16)
        for place, (_, span) in enumerate(groups[index]):
            attended_ref[:, span] = attended[place * tokens : (place + 1) * tokens]
        grad = jnp.where(living, grads[index].astype(jnp.float32) * inverse, 0.0).astype(jnp.bfloat16)
        return grad, jnp.sum(grad.astype(jnp.float32) * outputs, axis=1, keepdims=True)

    count = len(groups)
    scores, weights, sums, states, grad_weights, grad_scores = ([None] * count for _ in range(6))

    def score(index):
        scores[index] = contract(queries[index], key_rows[half:], (1, 1))

    def weigh(index):
        rows = slice(index * GROUP * tokens, (index + 1) * GROUP * tokens)
        weights[index] = exponentials(near_scores_ref[rows], scores[index])

    def attend(index):
        sums[index] = contract(weights[index], value_rows[...], (1, 0))

    def normalise(index):
        states[index] = normalised(index, sums[index])

    def grad_weigh(index):
        grad_weights[index] = contract(states[index][0], value_rows[:, :head_size], (1, 1))

    def grad_score(index):
        shifted = (grad_weights[index] - states[index][1]).astype(jnp.bfloat16)
        grad_scores[index] = weights[index] * shifted

    for step in range(count + 1):
        if step < count:
            score(step)
        if step > 0:
            weigh(step - 1)
            attend(step - 1)
    for step in range(count + 1):
        if step < count:
            normalise(step)
            grad_weigh(step)
        if step > 0:
            grad_score(step - 1)
    copy = pltpu.make_async_copy(attended_ref, attended_hbm, sem)
    copy.start()
    query = query_rows_ref[...]
    grad = jnp.concatenate([state[0] for state in states], axis=0)
    grad_rows_ref[...] = grad
    weights = jnp.concatenate(weights, axis=0)
    weights_ref[...] = weights
    grad_scores = jnp.concatenate(grad_scores, axis=0)
    grad_scores_ref[...] = grad_scores
    key_total = (contract(query, grad_scores[:, half:prompt], (0, 0)) * factor).astype(jnp.bfloat16).T
    value_total = contract(grad, weights[:, half:prompt], (0, 0)).astype(jnp.bfloat16).T
    for chip in range(chips):
        span = slice(chip * owned, (chip + 1) * owned)
        far_share_ref[chip, :, :head_size] = key_total[span]
        far_share_ref[chip, :, head_size:] = value_total[span]
    copy.wait()


def finish_kernel(
    query_rows_ref,
    weights_ref,
    grad_scores_ref,
    grad_rows_ref,
    key_rows,
    query_grad_hbm,
    key_grad_hbm,
    value_grad_hbm,
    near_share_ref,
    query_grad_ref,
    own_grad_ref,
    sems,
):
    tokens, head_size = own_grad_ref.shape[1:]
    half = near_share_ref.shape[0]
    prompt = 2 * half
    factor = 1.0 / math.sqrt(head_size)
    parts = head_parts(query_grad_ref.shape[1], tokens, head_size)
    copies = []

    def send(source, target):
        copy = pltpu.make_async_copy(source, target, sems.at[len(copies)])
        copy.start()
        copies.append(copy)

    query_grad = (contract(grad_scores_ref[...], key_rows[...], (1, 0)) * factor).astype(jnp.bfloat16)
    for rows, span in parts:
        query_grad_ref[:, span] = query_grad[rows]
    send(query_grad_ref, query_grad_hbm)
    query = query_rows_ref[...]
    operands = ((query, grad_scores_ref, factor), (grad_rows_ref[...], weights_ref, 1.0))
    for place, (rows, columns, scale) in enumerate(operands):
        own = contract(rows, columns[:, prompt:], (0, 0)) * scale
        own_grad_ref[place] = own.astype(jnp.bfloat16).T
        send(own_grad_ref.at[place], (key_grad_hbm, value_grad_hbm)[place])
    for place, (rows, columns, scale) in enumerate(operands):
        near = contract(rows, columns[:, :half], (0, 0)) * scale
        near_share_ref[:, place * head_size : (place + 1) * head_size] = near.T
    for copy in copies:
        copy.wait()


def join_kernel(near_share_ref, received_ref, out_ref):
    chips, owned, _ = out_ref.shape
    for chip in range(chips):
        near = near_share_ref[chip * owned : (chip + 1) * owned]
        out_ref[chip] = (near + received_ref[chip].astype(jnp.float32)).astype(jnp.bfloat16)


def on_device(ranks, queries, resp_keys, resp_values, prefix_keys, prefix_values, grad_out, lengths):
    tokens, columns = queries.shape[1:]
    owned, head_size = prefix_keys.shape
    key_count = ranks * owned + tokens
    half = jnp.bfloat16
    vmem = pl.BlockSpec(memory_space=pltpu.VMEM)
    anywhere = pl.BlockSpec(memory_space=pl.ANY)

    sent, living = pl.pallas_call(
        spread_kernel,
        out_shape=(
            pltpu.VMEM((ranks // 2, owned, 2 * head_size), half),
            pltpu.VMEM((tokens, head_size), jnp.float32),
        ),
        in_specs=[pl.BlockSpec(memory_space=pltpu.SMEM)] + [pl.BlockSpec(memory_space=pltpu.HBM)] * 2,
        out_specs=[vmem] * 2,
        scratch_shapes=[pltpu.VMEM((2, owned, head_size), half), pltpu.SemaphoreType.DMA((2,))],
    )(lengths, *(pltpu.with_memory_space_constraint(array, pltpu.HBM) for array in (prefix_keys, prefix_values)))
    same_core = [list(range(core, ranks, 2)) for core in range(2)]
    near = lax.all_to_all(sent, "roll", 0, 0, axis_index_groups=same_core)
    far = lax.ppermute(near, "roll", [(rank, rank ^ 1) for rank in range(ranks)])
    rows = columns // head_size * tokens
    hbm = pl.BlockSpec(memory_space=pltpu.HBM)
    stored = (queries[0], grad_out[0], resp_keys[0], resp_values[0])
    query_rows, grads, own, near_scores = pl.pallas_call(
        near_kernel,
        out_shape=(
            pltpu.VMEM((rows, head_size), half),
            pltpu.VMEM((tokens, columns), half),
            pltpu.VMEM((2, tokens, head_size), half),
            pltpu.VMEM((rows, ranks * owned // 2), jnp.float32),
        ),
        in_specs=[hbm] * 4 + [vmem],
        out_specs=[vmem] * 4,
        scratch_shapes=[pltpu.VMEM((tokens, columns), half), pltpu.SemaphoreType.DMA((4,))],
        compiler_params=pltpu.CompilerParams(vmem_limit_bytes=24 * 1024 * 1024),
        cost_estimate=pl.CostEstimate(
            flops=rows * ranks * owned * head_size, bytes_accessed=4 * rows * head_size, transcendentals=0
        ),
    )(*(pltpu.with_memory_space_constraint(array, pltpu.HBM) for array in stored), near)
    limit = pltpu.CompilerParams(vmem_limit_bytes=40 * 1024 * 1024)
    unit = 2 * rows * key_count * head_size
    chips = ranks // 2
    attended, weights, grad_scores, grad_rows, key_rows, far_share = pl.pallas_call(
        attention_kernel,
        out_shape=(
            jax.ShapeDtypeStruct((tokens, columns), half),
            pltpu.VMEM((rows, key_count), half),
            pltpu.VMEM((rows, key_count), half),
            pltpu.VMEM((rows, head_size), half),
            pltpu.VMEM((key_count, head_size), half),
            pltpu.VMEM((chips, owned, 2 * head_size), half),
        ),
        in_specs=[vmem] * 7,
        out_specs=[anywhere] + [vmem] * 5,
        scratch_shapes=[
            pltpu.VMEM((key_count, 2 * head_size), half),
            pltpu.VMEM((tokens, columns), half),
            pltpu.SemaphoreType.DMA,
        ],
        compiler_params=limit,
        cost_estimate=pl.CostEstimate(flops=5 * unit, bytes_accessed=4 * rows * columns, transcendentals=0),
    )(living, query_rows, grads, own, near, far, near_scores)
    received = lax.ppermute(far_share, "roll", [(rank, rank ^ 1) for rank in range(ranks)])
    query_grad, key_grad, value_grad, near_share = pl.pallas_call(
        finish_kernel,
        out_shape=(
            jax.ShapeDtypeStruct((tokens, columns), half),
            jax.ShapeDtypeStruct((tokens, head_size), half),
            jax.ShapeDtypeStruct((tokens, head_size), half),
            pltpu.VMEM((chips * owned, 2 * head_size), jnp.float32),
        ),
        in_specs=[vmem] * 5,
        out_specs=[anywhere] * 3 + [vmem],
        scratch_shapes=[
            pltpu.VMEM((tokens, columns), half),
            pltpu.VMEM((2, tokens, head_size), half),
            pltpu.SemaphoreType.DMA((3,)),
        ],
        compiler_params=limit,
        cost_estimate=pl.CostEstimate(flops=2 * unit, bytes_accessed=4 * rows * columns, transcendentals=0),
    )(query_rows, weights, grad_scores, grad_rows, key_rows)
    share = pl.pallas_call(
        join_kernel,
        out_shape=pltpu.VMEM((chips, owned, 2 * head_size), half),
        in_specs=[vmem] * 2,
        out_specs=vmem,
    )(near_share, received)
    pieces = lax.all_to_all(share, "roll", 0, 0, axis_index_groups=same_core)
    total = pieces[0].astype(jnp.float32)
    for chip in range(1, chips):
        total = total + pieces[chip].astype(jnp.float32)
    return (
        attended[None],
        query_grad[None],
        key_grad[None],
        value_grad[None],
        total[:, :head_size],
        total[:, head_size:],
    )


def solution(mesh):
    rolls = P(("prompt", "roll"), None, "head")
    prompts = P(("prompt", "roll"), "head")
    return jax.shard_map(
        functools.partial(on_device, mesh.shape["roll"]),
        mesh=mesh,
        in_specs=(rolls, rolls, rolls, prompts, prompts, rolls, P(("prompt", "roll"))),
        out_specs=(rolls, rolls, rolls, rolls, prompts, prompts),
        check_vma=False,
    )
```

```python
import functools
import math

import jax
import jax.numpy as jnp
from jax import lax
from jax.experimental import pallas as pl
from jax.experimental.pallas import tpu as pltpu
from jax.sharding import PartitionSpec as P

masked_score = -1e30
GROUP = 4


def contract(left, right, dims):
    return lax.dot_general(
        left, right, ((dims[:1], dims[1:]), ((), ())), preferred_element_type=jnp.float32
    )


def head_parts(columns, tokens, head_size):
    return [
        (slice(head * tokens, (head + 1) * tokens), slice(head * head_size, (head + 1) * head_size))
        for head in range(columns // head_size)
    ]


def spread_kernel(length_ref, key_hbm, value_hbm, out_ref, living_ref, own, sems):
    head_size = key_hbm.shape[1]
    copies = [
        pltpu.make_async_copy(source, own.at[place], sems.at[place])
        for place, source in enumerate((key_hbm, value_hbm))
    ]
    for copy in copies:
        copy.start()
    token = lax.broadcasted_iota(jnp.int32, living_ref.shape, 0)
    living_ref[...] = (token < length_ref[0]).astype(jnp.float32)
    for copy in copies:
        copy.wait()
    for place in range(out_ref.shape[0]):
        out_ref[place, :, :head_size] = own[0]
        out_ref[place, :, head_size:] = own[1]


def near_kernel(
    query_hbm,
    grad_hbm,
    resp_key_hbm,
    resp_value_hbm,
    near_ref,
    query_rows_ref,
    grad_ref,
    own_ref,
    scores_ref,
    query_ref,
    sems,
):
    tokens, head_size = own_ref.shape[1:]
    moves = (
        (query_hbm, query_ref),
        (grad_hbm, grad_ref),
        (resp_key_hbm, own_ref.at[0]),
        (resp_value_hbm, own_ref.at[1]),
    )
    copies = [
        pltpu.make_async_copy(source, target, sems.at[place])
        for place, (source, target) in enumerate(moves)
    ]
    for copy in copies:
        copy.start()
    keys = jnp.concatenate([near_ref[place, :, :head_size] for place in range(near_ref.shape[0])], axis=0)
    copies[0].wait()
    for rows, span in head_parts(query_ref.shape[1], tokens, head_size):
        query = query_ref[:, span]
        query_rows_ref[rows] = query
        scores_ref[rows] = contract(query, keys, (1, 1))
    for copy in copies[1:]:
        copy.wait()


def attention_kernel(
    living_ref,
    query_rows_ref,
    grad_ref,
    own_ref,
    near_ref,
    far_ref,
    near_scores_ref,
    attended_hbm,
    weights_ref,
    grad_scores_ref,
    grad_rows_ref,
    key_rows,
    far_share_ref,
    value_rows,
    attended_ref,
    sem,
):
    tokens, head_size = own_ref.shape[1:]
    chips, owned, _ = near_ref.shape
    half = chips * owned
    prompt = 2 * half
    heads = grad_ref.shape[1] // head_size
    factor = 1.0 / math.sqrt(head_size)
    exponent_factor = factor * math.log2(math.e)
    parts = head_parts(grad_ref.shape[1], tokens, head_size)
    for side, part_ref in enumerate((near_ref, far_ref)):
        for chip in range(chips):
            span = slice(side * half + chip * owned, side * half + (chip + 1) * owned)
            key_rows[span] = part_ref[chip, :, :head_size]
            value_rows[span, :head_size] = part_ref[chip, :, head_size:]
    key_rows[prompt:] = own_ref[0]
    value_rows[prompt:, :head_size] = own_ref[1]
    value_rows[:, head_size:] = jnp.ones((prompt + tokens, head_size), jnp.bfloat16)

    groups = [parts[at : at + GROUP] for at in range(0, heads, GROUP)]
    queries = [query_rows_ref[at * tokens : (at + GROUP) * tokens] for at in range(0, heads, GROUP)]
    grads = [jnp.concatenate([grad_ref[:, span] for _, span in group], axis=0) for group in groups]
    living = jnp.concatenate([living_ref[...]] * GROUP, axis=0) > 0.0
    token = lax.broadcasted_iota(jnp.int32, (GROUP * tokens, tokens), 0) % tokens
    allowed = lax.broadcasted_iota(jnp.int32, (GROUP * tokens, tokens), 1) <= token

    def exponentials(near, scores):
        own = jnp.where(allowed, scores[:, half:], masked_score)
        parts = (near, scores[:, :half], own)
        row_max = functools.reduce(jnp.maximum, [jnp.max(part, axis=1, keepdims=True) for part in parts])
        return jnp.concatenate(
            [jnp.exp2((part - row_max) * exponent_factor).astype(jnp.bfloat16) for part in parts], axis=1
        )

    def normalised(index, sums):
        inverse = 1.0 / sums[:, head_size:]
        outputs = sums[:, :head_size] * inverse
        attended = jnp.where(living, outputs, 0.0).astype(jnp.bfloat16)
        for place, (_, span) in enumerate(groups[index]):
            attended_ref[:, span] = attended[place * tokens : (place + 1) * tokens]
        grad = jnp.where(living, grads[index].astype(jnp.float32) * inverse, 0.0).astype(jnp.bfloat16)
        return grad, jnp.sum(grad.astype(jnp.float32) * outputs, axis=1, keepdims=True)

    count = len(groups)
    scores, weights, sums, states, grad_weights, grad_scores = ([None] * count for _ in range(6))

    def score(index):
        scores[index] = contract(queries[index], key_rows[half:], (1, 1))

    def weigh(index):
        rows = slice(index * GROUP * tokens, (index + 1) * GROUP * tokens)
        weights[index] = exponentials(near_scores_ref[rows], scores[index])

    def attend(index):
        sums[index] = contract(weights[index], value_rows[...], (1, 0))

    def normalise(index):
        states[index] = normalised(index, sums[index])

    def grad_weigh(index):
        grad_weights[index] = contract(states[index][0], value_rows[:, :head_size], (1, 1))

    def grad_score(index):
        shifted = (grad_weights[index] - states[index][1]).astype(jnp.bfloat16)
        grad_scores[index] = weights[index] * shifted

    for step in range(count + 1):
        if step < count:
            score(step)
        if step > 0:
            weigh(step - 1)
            attend(step - 1)
    for step in range(count + 1):
        if step < count:
            normalise(step)
            grad_weigh(step)
        if step > 0:
            grad_score(step - 1)
    copy = pltpu.make_async_copy(attended_ref, attended_hbm, sem)
    copy.start()
    query = query_rows_ref[...]
    grad = jnp.concatenate([state[0] for state in states], axis=0)
    grad_rows_ref[...] = grad
    weights = jnp.concatenate(weights, axis=0)
    weights_ref[...] = weights
    grad_scores = jnp.concatenate(grad_scores, axis=0)
    grad_scores_ref[...] = grad_scores
    key_total = (contract(query, grad_scores[:, half:prompt], (0, 0)) * factor).astype(jnp.bfloat16).T
    value_total = contract(grad, weights[:, half:prompt], (0, 0)).astype(jnp.bfloat16).T
    for chip in range(chips):
        span = slice(chip * owned, (chip + 1) * owned)
        far_share_ref[chip, :, :head_size] = key_total[span]
        far_share_ref[chip, :, head_size:] = value_total[span]
    copy.wait()


def finish_kernel(
    query_rows_ref,
    weights_ref,
    grad_scores_ref,
    grad_rows_ref,
    key_rows,
    query_grad_hbm,
    key_grad_hbm,
    value_grad_hbm,
    near_share_ref,
    query_grad_ref,
    own_grad_ref,
    sems,
):
    tokens, head_size = own_grad_ref.shape[1:]
    half = near_share_ref.shape[0]
    prompt = 2 * half
    factor = 1.0 / math.sqrt(head_size)
    parts = head_parts(query_grad_ref.shape[1], tokens, head_size)
    copies = []

    def send(source, target):
        copy = pltpu.make_async_copy(source, target, sems.at[len(copies)])
        copy.start()
        copies.append(copy)

    query_grad = (contract(grad_scores_ref[...], key_rows[...], (1, 0)) * factor).astype(jnp.bfloat16)
    for rows, span in parts:
        query_grad_ref[:, span] = query_grad[rows]
    send(query_grad_ref, query_grad_hbm)
    query = query_rows_ref[...]
    operands = ((query, grad_scores_ref, factor), (grad_rows_ref[...], weights_ref, 1.0))
    for place, (rows, columns, scale) in enumerate(operands):
        own = contract(rows, columns[:, prompt:], (0, 0)) * scale
        own_grad_ref[place] = own.astype(jnp.bfloat16).T
        send(own_grad_ref.at[place], (key_grad_hbm, value_grad_hbm)[place])
    for place, (rows, columns, scale) in enumerate(operands):
        near = contract(rows, columns[:, :half], (0, 0)) * scale
        near_share_ref[:, place * head_size : (place + 1) * head_size] = near.T
    for copy in copies:
        copy.wait()


def join_kernel(near_share_ref, received_ref, out_ref):
    chips, owned, _ = out_ref.shape
    for chip in range(chips):
        near = near_share_ref[chip * owned : (chip + 1) * owned]
        out_ref[chip] = (near + received_ref[chip].astype(jnp.float32)).astype(jnp.bfloat16)


def on_device(ranks, queries, resp_keys, resp_values, prefix_keys, prefix_values, grad_out, lengths):
    tokens, columns = queries.shape[1:]
    owned, head_size = prefix_keys.shape
    key_count = ranks * owned + tokens
    half = jnp.bfloat16
    vmem = pl.BlockSpec(memory_space=pltpu.VMEM)
    anywhere = pl.BlockSpec(memory_space=pl.ANY)

    sent, living = pl.pallas_call(
        spread_kernel,
        out_shape=(
            pltpu.VMEM((ranks // 2, owned, 2 * head_size), half),
            pltpu.VMEM((tokens, head_size), jnp.float32),
        ),
        in_specs=[pl.BlockSpec(memory_space=pltpu.SMEM)] + [pl.BlockSpec(memory_space=pltpu.HBM)] * 2,
        out_specs=[vmem] * 2,
        scratch_shapes=[pltpu.VMEM((2, owned, head_size), half), pltpu.SemaphoreType.DMA((2,))],
    )(lengths, *(pltpu.with_memory_space_constraint(array, pltpu.HBM) for array in (prefix_keys, prefix_values)))
    same_core = [list(range(core, ranks, 2)) for core in range(2)]
    near = lax.all_to_all(sent, "roll", 0, 0, axis_index_groups=same_core)
    far = lax.ppermute(near, "roll", [(rank, rank ^ 1) for rank in range(ranks)])
    rows = columns // head_size * tokens
    hbm = pl.BlockSpec(memory_space=pltpu.HBM)
    stored = (queries[0], grad_out[0], resp_keys[0], resp_values[0])
    query_rows, grads, own, near_scores = pl.pallas_call(
        near_kernel,
        out_shape=(
            pltpu.VMEM((rows, head_size), half),
            pltpu.VMEM((tokens, columns), half),
            pltpu.VMEM((2, tokens, head_size), half),
            pltpu.VMEM((rows, ranks * owned // 2), jnp.float32),
        ),
        in_specs=[hbm] * 4 + [vmem],
        out_specs=[vmem] * 4,
        scratch_shapes=[pltpu.VMEM((tokens, columns), half), pltpu.SemaphoreType.DMA((4,))],
        compiler_params=pltpu.CompilerParams(vmem_limit_bytes=24 * 1024 * 1024),
        cost_estimate=pl.CostEstimate(
            flops=rows * ranks * owned * head_size, bytes_accessed=4 * rows * head_size, transcendentals=0
        ),
    )(*(pltpu.with_memory_space_constraint(array, pltpu.HBM) for array in stored), near)
    limit = pltpu.CompilerParams(vmem_limit_bytes=40 * 1024 * 1024)
    unit = 2 * rows * key_count * head_size
    chips = ranks // 2
    attended, weights, grad_scores, grad_rows, key_rows, far_share = pl.pallas_call(
        attention_kernel,
        out_shape=(
            jax.ShapeDtypeStruct((tokens, columns), half),
            pltpu.VMEM((rows, key_count), half),
            pltpu.VMEM((rows, key_count), half),
            pltpu.VMEM((rows, head_size), half),
            pltpu.VMEM((key_count, head_size), half),
            pltpu.VMEM((chips, owned, 2 * head_size), half),
        ),
        in_specs=[vmem] * 7,
        out_specs=[anywhere] + [vmem] * 5,
        scratch_shapes=[
            pltpu.VMEM((key_count, 2 * head_size), half),
            pltpu.VMEM((tokens, columns), half),
            pltpu.SemaphoreType.DMA,
        ],
        compiler_params=limit,
        cost_estimate=pl.CostEstimate(flops=5 * unit, bytes_accessed=4 * rows * columns, transcendentals=0),
    )(living, query_rows, grads, own, near, far, near_scores)
    received = lax.ppermute(far_share, "roll", [(rank, rank ^ 1) for rank in range(ranks)])
    query_grad, key_grad, value_grad, near_share = pl.pallas_call(
        finish_kernel,
        out_shape=(
            jax.ShapeDtypeStruct((tokens, columns), half),
            jax.ShapeDtypeStruct((tokens, head_size), half),
            jax.ShapeDtypeStruct((tokens, head_size), half),
            pltpu.VMEM((chips * owned, 2 * head_size), jnp.float32),
        ),
        in_specs=[vmem] * 5,
        out_specs=[anywhere] * 3 + [vmem],
        scratch_shapes=[
            pltpu.VMEM((tokens, columns), half),
            pltpu.VMEM((2, tokens, head_size), half),
            pltpu.SemaphoreType.DMA((3,)),
        ],
        compiler_params=limit,
        cost_estimate=pl.CostEstimate(flops=2 * unit, bytes_accessed=4 * rows * columns, transcendentals=0),
    )(query_rows, weights, grad_scores, grad_rows, key_rows)
    share = pl.pallas_call(
        join_kernel,
        out_shape=pltpu.VMEM((chips, owned, 2 * head_size), half),
        in_specs=[vmem] * 2,
        out_specs=vmem,
        compiler_params=pltpu.CompilerParams(vmem_limit_bytes=8 * 1024 * 1024),
    )(near_share, received)
    pieces = lax.all_to_all(share, "roll", 0, 0, axis_index_groups=same_core)
    total = pieces[0].astype(jnp.float32)
    for chip in range(1, chips):
        total = total + pieces[chip].astype(jnp.float32)
    return (
        attended[None],
        query_grad[None],
        key_grad[None],
        value_grad[None],
        total[:, :head_size],
        total[:, head_size:],
    )


def solution(mesh):
    rolls = P(("prompt", "roll"), None, "head")
    prompts = P(("prompt", "roll"), "head")
    return jax.shard_map(
        functools.partial(on_device, mesh.shape["roll"]),
        mesh=mesh,
        in_specs=(rolls, rolls, rolls, prompts, prompts, rolls, P(("prompt", "roll"))),
        out_specs=(rolls, rolls, rolls, rolls, prompts, prompts),
        check_vma=False,
    )
```

```python
import functools
import math

import jax
import jax.numpy as jnp
from jax import lax
from jax.experimental import pallas as pl
from jax.experimental.pallas import tpu as pltpu
from jax.sharding import PartitionSpec as P

masked_score = -1e30
GROUP = 4


def contract(left, right, dims):
    return lax.dot_general(
        left, right, ((dims[:1], dims[1:]), ((), ())), preferred_element_type=jnp.float32
    )


def head_parts(columns, tokens, head_size):
    return [
        (slice(head * tokens, (head + 1) * tokens), slice(head * head_size, (head + 1) * head_size))
        for head in range(columns // head_size)
    ]


def spread_kernel(length_ref, key_hbm, value_hbm, out_ref, living_ref, own, sems):
    head_size = key_hbm.shape[1]
    copies = [
        pltpu.make_async_copy(source, own.at[place], sems.at[place])
        for place, source in enumerate((key_hbm, value_hbm))
    ]
    for copy in copies:
        copy.start()
    token = lax.broadcasted_iota(jnp.int32, living_ref.shape, 0)
    living_ref[...] = (token < length_ref[0]).astype(jnp.float32)
    for copy in copies:
        copy.wait()
    for place in range(out_ref.shape[0]):
        out_ref[place, :, :head_size] = own[0]
        out_ref[place, :, head_size:] = own[1]


def near_kernel(
    query_hbm,
    grad_hbm,
    resp_key_hbm,
    resp_value_hbm,
    near_ref,
    query_rows_ref,
    grad_ref,
    own_ref,
    scores_ref,
    query_ref,
    sems,
):
    tokens, head_size = own_ref.shape[1:]
    moves = (
        (query_hbm, query_ref),
        (grad_hbm, grad_ref),
        (resp_key_hbm, own_ref.at[0]),
        (resp_value_hbm, own_ref.at[1]),
    )
    copies = [
        pltpu.make_async_copy(source, target, sems.at[place])
        for place, (source, target) in enumerate(moves)
    ]
    for copy in copies:
        copy.start()
    keys = jnp.concatenate([near_ref[place, :, :head_size] for place in range(near_ref.shape[0])], axis=0)
    copies[0].wait()
    for rows, span in head_parts(query_ref.shape[1], tokens, head_size):
        query = query_ref[:, span]
        query_rows_ref[rows] = query
        scores_ref[rows] = contract(query, keys, (1, 1))
    for copy in copies[1:]:
        copy.wait()


def attention_kernel(
    living_ref,
    query_rows_ref,
    grad_ref,
    own_ref,
    near_ref,
    far_ref,
    near_scores_ref,
    attended_hbm,
    weights_ref,
    grad_scores_ref,
    grad_rows_ref,
    key_rows,
    far_share_ref,
    value_rows,
    attended_ref,
    sem,
):
    tokens, head_size = own_ref.shape[1:]
    chips, owned, _ = near_ref.shape
    half = chips * owned
    prompt = 2 * half
    heads = grad_ref.shape[1] // head_size
    factor = 1.0 / math.sqrt(head_size)
    exponent_factor = factor * math.log2(math.e)
    parts = head_parts(grad_ref.shape[1], tokens, head_size)
    for side, part_ref in enumerate((near_ref, far_ref)):
        for chip in range(chips):
            span = slice(side * half + chip * owned, side * half + (chip + 1) * owned)
            key_rows[span] = part_ref[chip, :, :head_size]
            value_rows[span, :head_size] = part_ref[chip, :, head_size:]
    key_rows[prompt:] = own_ref[0]
    value_rows[prompt:, :head_size] = own_ref[1]
    value_rows[:, head_size:] = jnp.ones((prompt + tokens, head_size), jnp.bfloat16)

    groups = [parts[at : at + GROUP] for at in range(0, heads, GROUP)]
    queries = [query_rows_ref[at * tokens : (at + GROUP) * tokens] for at in range(0, heads, GROUP)]
    grads = [jnp.concatenate([grad_ref[:, span] for _, span in group], axis=0) for group in groups]
    living = jnp.concatenate([living_ref[...]] * GROUP, axis=0) > 0.0
    token = lax.broadcasted_iota(jnp.int32, (GROUP * tokens, tokens), 0) % tokens
    allowed = lax.broadcasted_iota(jnp.int32, (GROUP * tokens, tokens), 1) <= token

    def exponentials(near, scores):
        own = jnp.where(allowed, scores[:, half:], masked_score)
        parts = (near, scores[:, :half], own)
        row_max = functools.reduce(jnp.maximum, [jnp.max(part, axis=1, keepdims=True) for part in parts])
        return jnp.concatenate(
            [jnp.exp2((part - row_max) * exponent_factor).astype(jnp.bfloat16) for part in parts], axis=1
        )

    def normalised(index, sums):
        inverse = 1.0 / sums[:, head_size:]
        outputs = sums[:, :head_size] * inverse
        attended = jnp.where(living, outputs, 0.0).astype(jnp.bfloat16)
        for place, (_, span) in enumerate(groups[index]):
            attended_ref[:, span] = attended[place * tokens : (place + 1) * tokens]
        grad = jnp.where(living, grads[index].astype(jnp.float32) * inverse, 0.0).astype(jnp.bfloat16)
        return grad, jnp.sum(grad.astype(jnp.float32) * outputs, axis=1, keepdims=True)

    count = len(groups)
    scores, weights, sums, states, grad_weights, grad_scores = ([None] * count for _ in range(6))

    def score(index):
        scores[index] = contract(queries[index], key_rows[half:], (1, 1))

    def weigh(index):
        rows = slice(index * GROUP * tokens, (index + 1) * GROUP * tokens)
        weights[index] = exponentials(near_scores_ref[rows], scores[index])

    def attend(index):
        sums[index] = contract(weights[index], value_rows[...], (1, 0))

    def normalise(index):
        states[index] = normalised(index, sums[index])

    def grad_weigh(index):
        grad_weights[index] = contract(states[index][0], value_rows[:, :head_size], (1, 1))

    def grad_score(index):
        shifted = (grad_weights[index] - states[index][1]).astype(jnp.bfloat16)
        grad_scores[index] = weights[index] * shifted

    for step in range(count + 1):
        if step < count:
            score(step)
        if step > 0:
            weigh(step - 1)
            attend(step - 1)
    for step in range(count + 1):
        if step < count:
            normalise(step)
            grad_weigh(step)
        if step > 0:
            grad_score(step - 1)
    copy = pltpu.make_async_copy(attended_ref, attended_hbm, sem)
    copy.start()
    query = query_rows_ref[...]
    grad = jnp.concatenate([state[0] for state in states], axis=0)
    grad_rows_ref[...] = grad
    weights = jnp.concatenate(weights, axis=0)
    weights_ref[...] = weights
    grad_scores = jnp.concatenate(grad_scores, axis=0)
    grad_scores_ref[...] = grad_scores
    key_total = (contract(query, grad_scores[:, half:prompt], (0, 0)) * factor).astype(jnp.bfloat16).T
    value_total = contract(grad, weights[:, half:prompt], (0, 0)).astype(jnp.bfloat16).T
    for chip in range(chips):
        span = slice(chip * owned, (chip + 1) * owned)
        far_share_ref[chip, :, :head_size] = key_total[span]
        far_share_ref[chip, :, head_size:] = value_total[span]
    copy.wait()


def finish_kernel(
    query_rows_ref,
    weights_ref,
    grad_scores_ref,
    grad_rows_ref,
    key_rows,
    query_grad_hbm,
    key_grad_hbm,
    value_grad_hbm,
    near_share_ref,
    query_grad_ref,
    own_grad_ref,
    sems,
):
    tokens, head_size = own_grad_ref.shape[1:]
    half = near_share_ref.shape[0]
    prompt = 2 * half
    factor = 1.0 / math.sqrt(head_size)
    parts = head_parts(query_grad_ref.shape[1], tokens, head_size)
    copies = []

    def send(source, target):
        copy = pltpu.make_async_copy(source, target, sems.at[len(copies)])
        copy.start()
        copies.append(copy)

    query = query_rows_ref[...]
    operands = ((query, grad_scores_ref, factor), (grad_rows_ref[...], weights_ref, 1.0))
    for place, (rows, columns, scale) in enumerate(operands):
        own = contract(rows, columns[:, prompt:], (0, 0)) * scale
        own_grad_ref[place] = own.astype(jnp.bfloat16).T
        send(own_grad_ref.at[place], (key_grad_hbm, value_grad_hbm)[place])
    for first in range(0, len(parts), GROUP):
        group = parts[first : first + GROUP]
        taken = slice(group[0][0].start, group[-1][0].stop)
        query_grad = contract(grad_scores_ref[taken], key_rows[...], (1, 0)) * factor
        for place, (_, span) in enumerate(group):
            query_grad_ref[:, span] = query_grad[place * tokens : (place + 1) * tokens].astype(jnp.bfloat16)
        lanes = slice(group[0][1].start, group[-1][1].stop)
        send(query_grad_ref.at[:, lanes], query_grad_hbm.at[:, lanes])
    for place, (rows, columns, scale) in enumerate(operands):
        near = contract(rows, columns[:, :half], (0, 0)) * scale
        near_share_ref[:, place * head_size : (place + 1) * head_size] = near.T
    for copy in copies:
        copy.wait()


def join_kernel(near_share_ref, received_ref, out_ref):
    chips, owned, _ = out_ref.shape
    for chip in range(chips):
        near = near_share_ref[chip * owned : (chip + 1) * owned]
        out_ref[chip] = (near + received_ref[chip].astype(jnp.float32)).astype(jnp.bfloat16)


def on_device(ranks, queries, resp_keys, resp_values, prefix_keys, prefix_values, grad_out, lengths):
    tokens, columns = queries.shape[1:]
    owned, head_size = prefix_keys.shape
    key_count = ranks * owned + tokens
    half = jnp.bfloat16
    vmem = pl.BlockSpec(memory_space=pltpu.VMEM)
    anywhere = pl.BlockSpec(memory_space=pl.ANY)

    sent, living = pl.pallas_call(
        spread_kernel,
        out_shape=(
            pltpu.VMEM((ranks // 2, owned, 2 * head_size), half),
            pltpu.VMEM((tokens, head_size), jnp.float32),
        ),
        in_specs=[pl.BlockSpec(memory_space=pltpu.SMEM)] + [pl.BlockSpec(memory_space=pltpu.HBM)] * 2,
        out_specs=[vmem] * 2,
        scratch_shapes=[pltpu.VMEM((2, owned, head_size), half), pltpu.SemaphoreType.DMA((2,))],
    )(lengths, *(pltpu.with_memory_space_constraint(array, pltpu.HBM) for array in (prefix_keys, prefix_values)))
    same_core = [list(range(core, ranks, 2)) for core in range(2)]
    near = lax.all_to_all(sent, "roll", 0, 0, axis_index_groups=same_core)
    far = lax.ppermute(near, "roll", [(rank, rank ^ 1) for rank in range(ranks)])
    rows = columns // head_size * tokens
    hbm = pl.BlockSpec(memory_space=pltpu.HBM)
    stored = (queries[0], grad_out[0], resp_keys[0], resp_values[0])
    query_rows, grads, own, near_scores = pl.pallas_call(
        near_kernel,
        out_shape=(
            pltpu.VMEM((rows, head_size), half),
            pltpu.VMEM((tokens, columns), half),
            pltpu.VMEM((2, tokens, head_size), half),
            pltpu.VMEM((rows, ranks * owned // 2), jnp.float32),
        ),
        in_specs=[hbm] * 4 + [vmem],
        out_specs=[vmem] * 4,
        scratch_shapes=[pltpu.VMEM((tokens, columns), half), pltpu.SemaphoreType.DMA((4,))],
        compiler_params=pltpu.CompilerParams(vmem_limit_bytes=24 * 1024 * 1024),
        cost_estimate=pl.CostEstimate(
            flops=rows * ranks * owned * head_size, bytes_accessed=4 * rows * head_size, transcendentals=0
        ),
    )(*(pltpu.with_memory_space_constraint(array, pltpu.HBM) for array in stored), near)
    limit = pltpu.CompilerParams(vmem_limit_bytes=40 * 1024 * 1024)
    unit = 2 * rows * key_count * head_size
    chips = ranks // 2
    attended, weights, grad_scores, grad_rows, key_rows, far_share = pl.pallas_call(
        attention_kernel,
        out_shape=(
            jax.ShapeDtypeStruct((tokens, columns), half),
            pltpu.VMEM((rows, key_count), half),
            pltpu.VMEM((rows, key_count), half),
            pltpu.VMEM((rows, head_size), half),
            pltpu.VMEM((key_count, head_size), half),
            pltpu.VMEM((chips, owned, 2 * head_size), half),
        ),
        in_specs=[vmem] * 7,
        out_specs=[anywhere] + [vmem] * 5,
        scratch_shapes=[
            pltpu.VMEM((key_count, 2 * head_size), half),
            pltpu.VMEM((tokens, columns), half),
            pltpu.SemaphoreType.DMA,
        ],
        compiler_params=limit,
        cost_estimate=pl.CostEstimate(flops=5 * unit, bytes_accessed=4 * rows * columns, transcendentals=0),
    )(living, query_rows, grads, own, near, far, near_scores)
    received = lax.ppermute(far_share, "roll", [(rank, rank ^ 1) for rank in range(ranks)])
    query_grad, key_grad, value_grad, near_share = pl.pallas_call(
        finish_kernel,
        out_shape=(
            jax.ShapeDtypeStruct((tokens, columns), half),
            jax.ShapeDtypeStruct((tokens, head_size), half),
            jax.ShapeDtypeStruct((tokens, head_size), half),
            pltpu.VMEM((chips * owned, 2 * head_size), jnp.float32),
        ),
        in_specs=[vmem] * 5,
        out_specs=[anywhere] * 3 + [vmem],
        scratch_shapes=[
            pltpu.VMEM((tokens, columns), half),
            pltpu.VMEM((2, tokens, head_size), half),
            pltpu.SemaphoreType.DMA((2 + rows // tokens // GROUP,)),
        ],
        compiler_params=limit,
        cost_estimate=pl.CostEstimate(flops=2 * unit, bytes_accessed=4 * rows * columns, transcendentals=0),
    )(query_rows, weights, grad_scores, grad_rows, key_rows)
    share = pl.pallas_call(
        join_kernel,
        out_shape=pltpu.VMEM((chips, owned, 2 * head_size), half),
        in_specs=[vmem] * 2,
        out_specs=vmem,
        compiler_params=pltpu.CompilerParams(vmem_limit_bytes=8 * 1024 * 1024),
    )(near_share, received)
    pieces = lax.all_to_all(share, "roll", 0, 0, axis_index_groups=same_core)
    total = pieces[0].astype(jnp.float32)
    for chip in range(1, chips):
        total = total + pieces[chip].astype(jnp.float32)
    return (
        attended[None],
        query_grad[None],
        key_grad[None],
        value_grad[None],
        total[:, :head_size],
        total[:, head_size:],
    )


def solution(mesh):
    rolls = P(("prompt", "roll"), None, "head")
    prompts = P(("prompt", "roll"), "head")
    return jax.shard_map(
        functools.partial(on_device, mesh.shape["roll"]),
        mesh=mesh,
        in_specs=(rolls, rolls, rolls, prompts, prompts, rolls, P(("prompt", "roll"))),
        out_specs=(rolls, rolls, rolls, rolls, prompts, prompts),
        check_vma=False,
    )
```

```python
import functools
import math

import jax
import jax.numpy as jnp
from jax import lax
from jax.experimental import pallas as pl
from jax.experimental.pallas import tpu as pltpu
from jax.sharding import PartitionSpec as P

masked_score = -1e30
GROUP = 4


def contract(left, right, dims):
    return lax.dot_general(
        left, right, ((dims[:1], dims[1:]), ((), ())), preferred_element_type=jnp.float32
    )


def head_parts(columns, tokens, head_size):
    return [
        (slice(head * tokens, (head + 1) * tokens), slice(head * head_size, (head + 1) * head_size))
        for head in range(columns // head_size)
    ]


def spread_kernel(length_ref, key_hbm, value_hbm, out_ref, living_ref, own, sems):
    head_size = key_hbm.shape[1]
    copies = [
        pltpu.make_async_copy(source, own.at[place], sems.at[place])
        for place, source in enumerate((key_hbm, value_hbm))
    ]
    for copy in copies:
        copy.start()
    token = lax.broadcasted_iota(jnp.int32, living_ref.shape, 0)
    living_ref[...] = (token < length_ref[0]).astype(jnp.float32)
    for copy in copies:
        copy.wait()
    for place in range(out_ref.shape[0]):
        out_ref[place, :, :head_size] = own[0]
        out_ref[place, :, head_size:] = own[1]


def near_kernel(
    query_hbm,
    grad_hbm,
    resp_key_hbm,
    resp_value_hbm,
    near_ref,
    query_rows_ref,
    grad_ref,
    own_ref,
    scores_ref,
    query_ref,
    sems,
):
    tokens, head_size = own_ref.shape[1:]
    moves = (
        (query_hbm, query_ref),
        (grad_hbm, grad_ref),
        (resp_key_hbm, own_ref.at[0]),
        (resp_value_hbm, own_ref.at[1]),
    )
    copies = [
        pltpu.make_async_copy(source, target, sems.at[place])
        for place, (source, target) in enumerate(moves)
    ]
    for copy in copies:
        copy.start()
    keys = jnp.concatenate([near_ref[place, :, :head_size] for place in range(near_ref.shape[0])], axis=0)
    copies[0].wait()
    for rows, span in head_parts(query_ref.shape[1], tokens, head_size):
        query = query_ref[:, span]
        query_rows_ref[rows] = query
        scores_ref[rows] = contract(query, keys, (1, 1))
    for copy in copies[1:]:
        copy.wait()


def attention_kernel(
    living_ref,
    query_rows_ref,
    grad_ref,
    own_ref,
    near_ref,
    far_ref,
    near_scores_ref,
    attended_hbm,
    weights_ref,
    grad_scores_ref,
    grad_rows_ref,
    key_rows,
    far_share_ref,
    value_rows,
    attended_ref,
    sem,
):
    tokens, head_size = own_ref.shape[1:]
    chips, owned, _ = near_ref.shape
    half = chips * owned
    prompt = 2 * half
    heads = grad_ref.shape[1] // head_size
    factor = 1.0 / math.sqrt(head_size)
    exponent_factor = factor * math.log2(math.e)
    parts = head_parts(grad_ref.shape[1], tokens, head_size)
    for side, part_ref in enumerate((near_ref, far_ref)):
        for chip in range(chips):
            span = slice(side * half + chip * owned, side * half + (chip + 1) * owned)
            key_rows[span] = part_ref[chip, :, :head_size]
            value_rows[span, :head_size] = part_ref[chip, :, head_size:]
    key_rows[prompt:] = own_ref[0]
    value_rows[prompt:, :head_size] = own_ref[1]
    value_rows[:, head_size:] = jnp.ones((prompt + tokens, head_size), jnp.bfloat16)

    groups = [parts[at : at + GROUP] for at in range(0, heads, GROUP)]
    queries = [query_rows_ref[at * tokens : (at + GROUP) * tokens] for at in range(0, heads, GROUP)]
    grads = [jnp.concatenate([grad_ref[:, span] for _, span in group], axis=0) for group in groups]
    living = jnp.concatenate([living_ref[...]] * GROUP, axis=0) > 0.0
    token = lax.broadcasted_iota(jnp.int32, (GROUP * tokens, tokens), 0) % tokens
    allowed = lax.broadcasted_iota(jnp.int32, (GROUP * tokens, tokens), 1) <= token

    def exponentials(near, scores):
        own = jnp.where(allowed, scores[:, half:], masked_score)
        parts = (near, scores[:, :half], own)
        row_max = functools.reduce(jnp.maximum, [jnp.max(part, axis=1, keepdims=True) for part in parts])
        return jnp.concatenate(
            [jnp.exp2((part - row_max) * exponent_factor).astype(jnp.bfloat16) for part in parts], axis=1
        )

    def normalised(index, sums):
        inverse = 1.0 / sums[:, head_size:]
        outputs = sums[:, :head_size] * inverse
        attended = jnp.where(living, outputs, 0.0).astype(jnp.bfloat16)
        for place, (_, span) in enumerate(groups[index]):
            attended_ref[:, span] = attended[place * tokens : (place + 1) * tokens]
        grad = jnp.where(living, grads[index].astype(jnp.float32) * inverse, 0.0).astype(jnp.bfloat16)
        return grad, jnp.sum(grad.astype(jnp.float32) * outputs, axis=1, keepdims=True)

    count = len(groups)
    scores, weights, sums, states, grad_weights, grad_scores = ([None] * count for _ in range(6))

    def score(index):
        scores[index] = contract(queries[index], key_rows[half:], (1, 1))

    def weigh(index):
        rows = slice(index * GROUP * tokens, (index + 1) * GROUP * tokens)
        weights[index] = exponentials(near_scores_ref[rows], scores[index])

    def attend(index):
        sums[index] = contract(weights[index], value_rows[...], (1, 0))

    def normalise(index):
        states[index] = normalised(index, sums[index])

    def grad_weigh(index):
        grad_weights[index] = contract(states[index][0], value_rows[:, :head_size], (1, 1))

    def grad_score(index):
        shifted = (grad_weights[index] - states[index][1]).astype(jnp.bfloat16)
        grad_scores[index] = weights[index] * shifted

    for step in range(count + 1):
        if step < count:
            score(step)
        if step > 0:
            weigh(step - 1)
            attend(step - 1)
    for step in range(count + 1):
        if step < count:
            normalise(step)
            grad_weigh(step)
        if step == count - 1:
            copy = pltpu.make_async_copy(attended_ref, attended_hbm, sem)
            copy.start()
        if step > 0:
            grad_score(step - 1)
    query = query_rows_ref[...]
    grad = jnp.concatenate([state[0] for state in states], axis=0)
    grad_rows_ref[...] = grad
    weights = jnp.concatenate(weights, axis=0)
    weights_ref[...] = weights
    grad_scores = jnp.concatenate(grad_scores, axis=0)
    grad_scores_ref[...] = grad_scores
    key_total = (contract(query, grad_scores[:, half:prompt], (0, 0)) * factor).astype(jnp.bfloat16).T
    value_total = contract(grad, weights[:, half:prompt], (0, 0)).astype(jnp.bfloat16).T
    for chip in range(chips):
        span = slice(chip * owned, (chip + 1) * owned)
        far_share_ref[chip, :, :head_size] = key_total[span]
        far_share_ref[chip, :, head_size:] = value_total[span]
    copy.wait()


def finish_kernel(
    query_rows_ref,
    weights_ref,
    grad_scores_ref,
    grad_rows_ref,
    key_rows,
    query_grad_hbm,
    key_grad_hbm,
    value_grad_hbm,
    near_share_ref,
    query_grad_ref,
    own_grad_ref,
    sems,
):
    tokens, head_size = own_grad_ref.shape[1:]
    half = near_share_ref.shape[0]
    prompt = 2 * half
    factor = 1.0 / math.sqrt(head_size)
    parts = head_parts(query_grad_ref.shape[1], tokens, head_size)
    copies = []

    def send(source, target):
        copy = pltpu.make_async_copy(source, target, sems.at[len(copies)])
        copy.start()
        copies.append(copy)

    query = query_rows_ref[...]
    operands = ((query, grad_scores_ref, factor), (grad_rows_ref[...], weights_ref, 1.0))
    for place, (rows, columns, scale) in enumerate(operands):
        own = contract(rows, columns[:, prompt:], (0, 0)) * scale
        own_grad_ref[place] = own.astype(jnp.bfloat16).T
        send(own_grad_ref.at[place], (key_grad_hbm, value_grad_hbm)[place])
    for first in range(0, len(parts), GROUP):
        group = parts[first : first + GROUP]
        taken = slice(group[0][0].start, group[-1][0].stop)
        query_grad = contract(grad_scores_ref[taken], key_rows[...], (1, 0)) * factor
        for place, (_, span) in enumerate(group):
            query_grad_ref[:, span] = query_grad[place * tokens : (place + 1) * tokens].astype(jnp.bfloat16)
        lanes = slice(group[0][1].start, group[-1][1].stop)
        send(query_grad_ref.at[:, lanes], query_grad_hbm.at[:, lanes])
    for place, (rows, columns, scale) in enumerate(operands):
        near = contract(rows, columns[:, :half], (0, 0)) * scale
        near_share_ref[:, place * head_size : (place + 1) * head_size] = near.T
    for copy in copies:
        copy.wait()


def join_kernel(near_share_ref, received_ref, out_ref):
    chips, owned, _ = out_ref.shape
    for chip in range(chips):
        near = near_share_ref[chip * owned : (chip + 1) * owned]
        out_ref[chip] = (near + received_ref[chip].astype(jnp.float32)).astype(jnp.bfloat16)


def on_device(ranks, queries, resp_keys, resp_values, prefix_keys, prefix_values, grad_out, lengths):
    tokens, columns = queries.shape[1:]
    owned, head_size = prefix_keys.shape
    key_count = ranks * owned + tokens
    half = jnp.bfloat16
    vmem = pl.BlockSpec(memory_space=pltpu.VMEM)
    anywhere = pl.BlockSpec(memory_space=pl.ANY)

    sent, living = pl.pallas_call(
        spread_kernel,
        out_shape=(
            pltpu.VMEM((ranks // 2, owned, 2 * head_size), half),
            pltpu.VMEM((tokens, head_size), jnp.float32),
        ),
        in_specs=[pl.BlockSpec(memory_space=pltpu.SMEM)] + [pl.BlockSpec(memory_space=pltpu.HBM)] * 2,
        out_specs=[vmem] * 2,
        scratch_shapes=[pltpu.VMEM((2, owned, head_size), half), pltpu.SemaphoreType.DMA((2,))],
    )(lengths, *(pltpu.with_memory_space_constraint(array, pltpu.HBM) for array in (prefix_keys, prefix_values)))
    same_core = [list(range(core, ranks, 2)) for core in range(2)]
    near = lax.all_to_all(sent, "roll", 0, 0, axis_index_groups=same_core)
    far = lax.ppermute(near, "roll", [(rank, rank ^ 1) for rank in range(ranks)])
    rows = columns // head_size * tokens
    hbm = pl.BlockSpec(memory_space=pltpu.HBM)
    stored = (queries[0], grad_out[0], resp_keys[0], resp_values[0])
    query_rows, grads, own, near_scores = pl.pallas_call(
        near_kernel,
        out_shape=(
            pltpu.VMEM((rows, head_size), half),
            pltpu.VMEM((tokens, columns), half),
            pltpu.VMEM((2, tokens, head_size), half),
            pltpu.VMEM((rows, ranks * owned // 2), jnp.float32),
        ),
        in_specs=[hbm] * 4 + [vmem],
        out_specs=[vmem] * 4,
        scratch_shapes=[pltpu.VMEM((tokens, columns), half), pltpu.SemaphoreType.DMA((4,))],
        compiler_params=pltpu.CompilerParams(vmem_limit_bytes=24 * 1024 * 1024),
        cost_estimate=pl.CostEstimate(
            flops=rows * ranks * owned * head_size, bytes_accessed=4 * rows * head_size, transcendentals=0
        ),
    )(*(pltpu.with_memory_space_constraint(array, pltpu.HBM) for array in stored), near)
    limit = pltpu.CompilerParams(vmem_limit_bytes=40 * 1024 * 1024)
    unit = 2 * rows * key_count * head_size
    chips = ranks // 2
    attended, weights, grad_scores, grad_rows, key_rows, far_share = pl.pallas_call(
        attention_kernel,
        out_shape=(
            jax.ShapeDtypeStruct((tokens, columns), half),
            pltpu.VMEM((rows, key_count), half),
            pltpu.VMEM((rows, key_count), half),
            pltpu.VMEM((rows, head_size), half),
            pltpu.VMEM((key_count, head_size), half),
            pltpu.VMEM((chips, owned, 2 * head_size), half),
        ),
        in_specs=[vmem] * 7,
        out_specs=[anywhere] + [vmem] * 5,
        scratch_shapes=[
            pltpu.VMEM((key_count, 2 * head_size), half),
            pltpu.VMEM((tokens, columns), half),
            pltpu.SemaphoreType.DMA,
        ],
        compiler_params=limit,
        cost_estimate=pl.CostEstimate(flops=5 * unit, bytes_accessed=4 * rows * columns, transcendentals=0),
    )(living, query_rows, grads, own, near, far, near_scores)
    received = lax.ppermute(far_share, "roll", [(rank, rank ^ 1) for rank in range(ranks)])
    query_grad, key_grad, value_grad, near_share = pl.pallas_call(
        finish_kernel,
        out_shape=(
            jax.ShapeDtypeStruct((tokens, columns), half),
            jax.ShapeDtypeStruct((tokens, head_size), half),
            jax.ShapeDtypeStruct((tokens, head_size), half),
            pltpu.VMEM((chips * owned, 2 * head_size), jnp.float32),
        ),
        in_specs=[vmem] * 5,
        out_specs=[anywhere] * 3 + [vmem],
        scratch_shapes=[
            pltpu.VMEM((tokens, columns), half),
            pltpu.VMEM((2, tokens, head_size), half),
            pltpu.SemaphoreType.DMA((2 + rows // tokens // GROUP,)),
        ],
        compiler_params=limit,
        cost_estimate=pl.CostEstimate(flops=2 * unit, bytes_accessed=4 * rows * columns, transcendentals=0),
    )(query_rows, weights, grad_scores, grad_rows, key_rows)
    share = pl.pallas_call(
        join_kernel,
        out_shape=pltpu.VMEM((chips, owned, 2 * head_size), half),
        in_specs=[vmem] * 2,
        out_specs=vmem,
        compiler_params=pltpu.CompilerParams(vmem_limit_bytes=8 * 1024 * 1024),
    )(near_share, received)
    pieces = lax.all_to_all(share, "roll", 0, 0, axis_index_groups=same_core)
    total = pieces[0].astype(jnp.float32)
    for chip in range(1, chips):
        total = total + pieces[chip].astype(jnp.float32)
    return (
        attended[None],
        query_grad[None],
        key_grad[None],
        value_grad[None],
        total[:, :head_size],
        total[:, head_size:],
    )


def solution(mesh):
    rolls = P(("prompt", "roll"), None, "head")
    prompts = P(("prompt", "roll"), "head")
    return jax.shard_map(
        functools.partial(on_device, mesh.shape["roll"]),
        mesh=mesh,
        in_specs=(rolls, rolls, rolls, prompts, prompts, rolls, P(("prompt", "roll"))),
        out_specs=(rolls, rolls, rolls, rolls, prompts, prompts),
        check_vma=False,
    )
```

```python
import functools
import math

import jax
import jax.numpy as jnp
from jax import lax
from jax.experimental import pallas as pl
from jax.experimental.pallas import tpu as pltpu
from jax.sharding import PartitionSpec as P

masked_score = -1e30
GROUP = 4


def contract(left, right, dims):
    return lax.dot_general(
        left, right, ((dims[:1], dims[1:]), ((), ())), preferred_element_type=jnp.float32
    )


def head_parts(columns, tokens, head_size):
    return [
        (slice(head * tokens, (head + 1) * tokens), slice(head * head_size, (head + 1) * head_size))
        for head in range(columns // head_size)
    ]


def spread_kernel(
    key_hbm,
    value_hbm,
    query_hbm,
    grad_hbm,
    resp_key_hbm,
    resp_value_hbm,
    out_ref,
    query_ref,
    grad_ref,
    own_ref,
    prompt_own,
    sems,
):
    head_size = key_hbm.shape[1]
    moves = (
        (key_hbm, prompt_own.at[0]),
        (value_hbm, prompt_own.at[1]),
        (query_hbm, query_ref),
        (grad_hbm, grad_ref),
        (resp_key_hbm, own_ref.at[0]),
        (resp_value_hbm, own_ref.at[1]),
    )
    copies = [
        pltpu.make_async_copy(source, target, sems.at[place])
        for place, (source, target) in enumerate(moves)
    ]
    for copy in copies:
        copy.start()
    for copy in copies[:2]:
        copy.wait()
    for place in range(out_ref.shape[0]):
        out_ref[place, :, :head_size] = prompt_own[0]
        out_ref[place, :, head_size:] = prompt_own[1]
    for copy in copies[2:]:
        copy.wait()


def near_kernel(length_ref, query_ref, near_ref, query_rows_ref, scores_ref, living_ref):
    tokens = query_ref.shape[0]
    head_size = query_rows_ref.shape[1]
    token = lax.broadcasted_iota(jnp.int32, living_ref.shape, 0)
    living_ref[...] = (token < length_ref[0]).astype(jnp.float32)
    keys = jnp.concatenate([near_ref[place, :, :head_size] for place in range(near_ref.shape[0])], axis=0)
    for rows, span in head_parts(query_ref.shape[1], tokens, head_size):
        query = query_ref[:, span]
        query_rows_ref[rows] = query
        scores_ref[rows] = contract(query, keys, (1, 1))


def attention_kernel(
    living_ref,
    query_rows_ref,
    grad_ref,
    own_ref,
    near_ref,
    far_ref,
    near_scores_ref,
    attended_hbm,
    weights_ref,
    grad_scores_ref,
    grad_rows_ref,
    key_rows,
    far_share_ref,
    value_rows,
    attended_ref,
    sem,
):
    tokens, head_size = own_ref.shape[1:]
    chips, owned, _ = near_ref.shape
    half = chips * owned
    prompt = 2 * half
    heads = grad_ref.shape[1] // head_size
    factor = 1.0 / math.sqrt(head_size)
    exponent_factor = factor * math.log2(math.e)
    parts = head_parts(grad_ref.shape[1], tokens, head_size)
    for side, part_ref in enumerate((near_ref, far_ref)):
        for chip in range(chips):
            span = slice(side * half + chip * owned, side * half + (chip + 1) * owned)
            key_rows[span] = part_ref[chip, :, :head_size]
            value_rows[span, :head_size] = part_ref[chip, :, head_size:]
    key_rows[prompt:] = own_ref[0]
    value_rows[prompt:, :head_size] = own_ref[1]
    value_rows[:, head_size:] = jnp.ones((prompt + tokens, head_size), jnp.bfloat16)

    groups = [parts[at : at + GROUP] for at in range(0, heads, GROUP)]
    queries = [query_rows_ref[at * tokens : (at + GROUP) * tokens] for at in range(0, heads, GROUP)]
    grads = [jnp.concatenate([grad_ref[:, span] for _, span in group], axis=0) for group in groups]
    living = jnp.concatenate([living_ref[...]] * GROUP, axis=0) > 0.0
    token = lax.broadcasted_iota(jnp.int32, (GROUP * tokens, tokens), 0) % tokens
    allowed = lax.broadcasted_iota(jnp.int32, (GROUP * tokens, tokens), 1) <= token

    def exponentials(near, scores):
        own = jnp.where(allowed, scores[:, half:], masked_score)
        parts = (near, scores[:, :half], own)
        row_max = functools.reduce(jnp.maximum, [jnp.max(part, axis=1, keepdims=True) for part in parts])
        return jnp.concatenate(
            [jnp.exp2((part - row_max) * exponent_factor).astype(jnp.bfloat16) for part in parts], axis=1
        )

    def normalised(index, sums):
        inverse = 1.0 / sums[:, head_size:]
        outputs = sums[:, :head_size] * inverse
        attended = jnp.where(living, outputs, 0.0).astype(jnp.bfloat16)
        for place, (_, span) in enumerate(groups[index]):
            attended_ref[:, span] = attended[place * tokens : (place + 1) * tokens]
        grad = jnp.where(living, grads[index].astype(jnp.float32) * inverse, 0.0).astype(jnp.bfloat16)
        return grad, jnp.sum(grad.astype(jnp.float32) * outputs, axis=1, keepdims=True)

    count = len(groups)
    scores, weights, sums, states, grad_weights, grad_scores = ([None] * count for _ in range(6))

    def score(index):
        scores[index] = contract(queries[index], key_rows[half:], (1, 1))

    def weigh(index):
        rows = slice(index * GROUP * tokens, (index + 1) * GROUP * tokens)
        weights[index] = exponentials(near_scores_ref[rows], scores[index])

    def attend(index):
        sums[index] = contract(weights[index], value_rows[...], (1, 0))

    def normalise(index):
        states[index] = normalised(index, sums[index])

    def grad_weigh(index):
        grad_weights[index] = contract(states[index][0], value_rows[:, :head_size], (1, 1))

    def grad_score(index):
        shifted = (grad_weights[index] - states[index][1]).astype(jnp.bfloat16)
        grad_scores[index] = weights[index] * shifted

    for step in range(count + 1):
        if step < count:
            score(step)
        if step > 0:
            weigh(step - 1)
            attend(step - 1)
    for step in range(count + 1):
        if step < count:
            normalise(step)
            grad_weigh(step)
        if step > 0:
            grad_score(step - 1)
    copy = pltpu.make_async_copy(attended_ref, attended_hbm, sem)
    copy.start()
    query = query_rows_ref[...]
    grad = jnp.concatenate([state[0] for state in states], axis=0)
    grad_rows_ref[...] = grad
    weights = jnp.concatenate(weights, axis=0)
    weights_ref[...] = weights
    grad_scores = jnp.concatenate(grad_scores, axis=0)
    grad_scores_ref[...] = grad_scores
    key_total = (contract(query, grad_scores[:, half:prompt], (0, 0)) * factor).astype(jnp.bfloat16).T
    value_total = contract(grad, weights[:, half:prompt], (0, 0)).astype(jnp.bfloat16).T
    for chip in range(chips):
        span = slice(chip * owned, (chip + 1) * owned)
        far_share_ref[chip, :, :head_size] = key_total[span]
        far_share_ref[chip, :, head_size:] = value_total[span]
    copy.wait()


def finish_kernel(
    query_rows_ref,
    weights_ref,
    grad_scores_ref,
    grad_rows_ref,
    key_rows,
    query_grad_hbm,
    key_grad_hbm,
    value_grad_hbm,
    near_share_ref,
    query_grad_ref,
    own_grad_ref,
    sems,
):
    tokens, head_size = own_grad_ref.shape[1:]
    half = near_share_ref.shape[0]
    prompt = 2 * half
    factor = 1.0 / math.sqrt(head_size)
    parts = head_parts(query_grad_ref.shape[1], tokens, head_size)
    copies = []

    def send(source, target):
        copy = pltpu.make_async_copy(source, target, sems.at[len(copies)])
        copy.start()
        copies.append(copy)

    query = query_rows_ref[...]
    operands = ((query, grad_scores_ref, factor), (grad_rows_ref[...], weights_ref, 1.0))
    for place, (rows, columns, scale) in enumerate(operands):
        own = contract(rows, columns[:, prompt:], (0, 0)) * scale
        own_grad_ref[place] = own.astype(jnp.bfloat16).T
        send(own_grad_ref.at[place], (key_grad_hbm, value_grad_hbm)[place])
    for first in range(0, len(parts), GROUP):
        group = parts[first : first + GROUP]
        taken = slice(group[0][0].start, group[-1][0].stop)
        query_grad = contract(grad_scores_ref[taken], key_rows[...], (1, 0)) * factor
        for place, (_, span) in enumerate(group):
            query_grad_ref[:, span] = query_grad[place * tokens : (place + 1) * tokens].astype(jnp.bfloat16)
        lanes = slice(group[0][1].start, group[-1][1].stop)
        send(query_grad_ref.at[:, lanes], query_grad_hbm.at[:, lanes])
    for place, (rows, columns, scale) in enumerate(operands):
        near = contract(rows, columns[:, :half], (0, 0)) * scale
        near_share_ref[:, place * head_size : (place + 1) * head_size] = near.T
    for copy in copies:
        copy.wait()


def join_kernel(near_share_ref, received_ref, out_ref):
    chips, owned, _ = out_ref.shape
    for chip in range(chips):
        near = near_share_ref[chip * owned : (chip + 1) * owned]
        out_ref[chip] = (near + received_ref[chip].astype(jnp.float32)).astype(jnp.bfloat16)


def on_device(ranks, queries, resp_keys, resp_values, prefix_keys, prefix_values, grad_out, lengths):
    tokens, columns = queries.shape[1:]
    owned, head_size = prefix_keys.shape
    key_count = ranks * owned + tokens
    half = jnp.bfloat16
    vmem = pl.BlockSpec(memory_space=pltpu.VMEM)
    anywhere = pl.BlockSpec(memory_space=pl.ANY)

    hbm = pl.BlockSpec(memory_space=pltpu.HBM)
    stored = (prefix_keys, prefix_values, queries[0], grad_out[0], resp_keys[0], resp_values[0])
    sent, query, grads, own = pl.pallas_call(
        spread_kernel,
        out_shape=(
            pltpu.VMEM((ranks // 2, owned, 2 * head_size), half),
            pltpu.VMEM((tokens, columns), half),
            pltpu.VMEM((tokens, columns), half),
            pltpu.VMEM((2, tokens, head_size), half),
        ),
        in_specs=[hbm] * 6,
        out_specs=[vmem] * 4,
        scratch_shapes=[pltpu.VMEM((2, owned, head_size), half), pltpu.SemaphoreType.DMA((6,))],
        compiler_params=pltpu.CompilerParams(vmem_limit_bytes=8 * 1024 * 1024),
    )(*(pltpu.with_memory_space_constraint(array, pltpu.HBM) for array in stored))
    same_core = [list(range(core, ranks, 2)) for core in range(2)]
    near = lax.all_to_all(sent, "roll", 0, 0, axis_index_groups=same_core)
    far = lax.ppermute(near, "roll", [(rank, rank ^ 1) for rank in range(ranks)])
    rows = columns // head_size * tokens
    query_rows, near_scores, living = pl.pallas_call(
        near_kernel,
        out_shape=(
            pltpu.VMEM((rows, head_size), half),
            pltpu.VMEM((rows, ranks * owned // 2), jnp.float32),
            pltpu.VMEM((tokens, head_size), jnp.float32),
        ),
        in_specs=[pl.BlockSpec(memory_space=pltpu.SMEM)] + [vmem] * 2,
        out_specs=[vmem] * 3,
        compiler_params=pltpu.CompilerParams(vmem_limit_bytes=24 * 1024 * 1024),
        cost_estimate=pl.CostEstimate(
            flops=rows * ranks * owned * head_size, bytes_accessed=4 * rows * head_size, transcendentals=0
        ),
    )(lengths, query, near)
    limit = pltpu.CompilerParams(vmem_limit_bytes=40 * 1024 * 1024)
    unit = 2 * rows * key_count * head_size
    chips = ranks // 2
    attended, weights, grad_scores, grad_rows, key_rows, far_share = pl.pallas_call(
        attention_kernel,
        out_shape=(
            jax.ShapeDtypeStruct((tokens, columns), half),
            pltpu.VMEM((rows, key_count), half),
            pltpu.VMEM((rows, key_count), half),
            pltpu.VMEM((rows, head_size), half),
            pltpu.VMEM((key_count, head_size), half),
            pltpu.VMEM((chips, owned, 2 * head_size), half),
        ),
        in_specs=[vmem] * 7,
        out_specs=[anywhere] + [vmem] * 5,
        scratch_shapes=[
            pltpu.VMEM((key_count, 2 * head_size), half),
            pltpu.VMEM((tokens, columns), half),
            pltpu.SemaphoreType.DMA,
        ],
        compiler_params=limit,
        cost_estimate=pl.CostEstimate(flops=5 * unit, bytes_accessed=4 * rows * columns, transcendentals=0),
    )(living, query_rows, grads, own, near, far, near_scores)
    received = lax.ppermute(far_share, "roll", [(rank, rank ^ 1) for rank in range(ranks)])
    query_grad, key_grad, value_grad, near_share = pl.pallas_call(
        finish_kernel,
        out_shape=(
            jax.ShapeDtypeStruct((tokens, columns), half),
            jax.ShapeDtypeStruct((tokens, head_size), half),
            jax.ShapeDtypeStruct((tokens, head_size), half),
            pltpu.VMEM((chips * owned, 2 * head_size), jnp.float32),
        ),
        in_specs=[vmem] * 5,
        out_specs=[anywhere] * 3 + [vmem],
        scratch_shapes=[
            pltpu.VMEM((tokens, columns), half),
            pltpu.VMEM((2, tokens, head_size), half),
            pltpu.SemaphoreType.DMA((2 + rows // tokens // GROUP,)),
        ],
        compiler_params=limit,
        cost_estimate=pl.CostEstimate(flops=2 * unit, bytes_accessed=4 * rows * columns, transcendentals=0),
    )(query_rows, weights, grad_scores, grad_rows, key_rows)
    share = pl.pallas_call(
        join_kernel,
        out_shape=pltpu.VMEM((chips, owned, 2 * head_size), half),
        in_specs=[vmem] * 2,
        out_specs=vmem,
        compiler_params=pltpu.CompilerParams(vmem_limit_bytes=8 * 1024 * 1024),
    )(near_share, received)
    pieces = lax.all_to_all(share, "roll", 0, 0, axis_index_groups=same_core)
    total = pieces[0].astype(jnp.float32)
    for chip in range(1, chips):
        total = total + pieces[chip].astype(jnp.float32)
    return (
        attended[None],
        query_grad[None],
        key_grad[None],
        value_grad[None],
        total[:, :head_size],
        total[:, head_size:],
    )


def solution(mesh):
    rolls = P(("prompt", "roll"), None, "head")
    prompts = P(("prompt", "roll"), "head")
    return jax.shard_map(
        functools.partial(on_device, mesh.shape["roll"]),
        mesh=mesh,
        in_specs=(rolls, rolls, rolls, prompts, prompts, rolls, P(("prompt", "roll"))),
        out_specs=(rolls, rolls, rolls, rolls, prompts, prompts),
        check_vma=False,
    )
```
